32 devices in a mesh: fsdp: 8 (over z, core), frame: 4 (over y, x).
Axes of the slice: x: 2, y: 2, z: 4, core: 2. Of those that a mesh axis runs over, the one named last changes fastest.
Arguments:
- frames: bfloat16 [8, 1536, 3072], P('fsdp', 'frame'), may hold values from -6 to 6
- modulation: float32 [8, 2, 3072], P('fsdp'), may hold values from -3 to 3
- w_qkv: bfloat16 [3072, 768], P('fsdp'), may hold values from -0.109375 to 0.109375
- qk_gain: float32 [2, 128], replicated, may hold values from 0.1 to 1.9
- w_out: bfloat16 [256, 3072], P(None, 'fsdp'), may hold values from -0.375 to 0.375
Outputs:
- mixed: bfloat16 [8, 1536, 3072], P('fsdp', 'frame')
The draws below stay inside these ranges and needn't reach their ends.
All inputs are finite; a program needn't handle non-finite values.
Results may differ from the reference program's by a relative error of at most 0.0053.
Values may be sent and summed in bfloat16 or wider, within the bound.
No kernel may reach another device: no remote copies, remote signals or barrier semaphores. Data moves between devices by JAX's collectives and lax.ppermute only.
A program may use at most 64 MiB of HBM per device.

```python
import math
import jax
import jax.numpy as jnp
from jax import lax

D = 3072
HEAD_DIM = 128
HEADS = 2
TILE = 128
REACH = 2
BORDER = 256
WINDOW = 640
VIDEOS = 8
FRAME_TOK = 1536
TILES = 12


def block_scale(stream_key, shape, split, low, high):
    loudness = 1.0
    for dim, blocks in split:
        heights = jax.random.uniform(jax.random.fold_in(jax.random.fold_in(stream_key, 6), dim), (blocks,), jnp.float32, low / len(split), high / len(split))
        loudness = loudness * jnp.repeat(jnp.exp(heights), shape[dim] // blocks).reshape((-1,) + (1,) * (len(shape) - 1 - dim))
    return loudness


def normal_values(key, extent, deviation, bound, cuts=(), kind=jnp.bfloat16):
    factor_of = block_scale(key, extent, cuts, -0.22, 0.18) if cuts else 1.0
    array = jax.random.normal(key, extent, jnp.float32) * deviation * factor_of
    return jnp.minimum(jnp.maximum(array, -bound), bound).astype(kind)


def setup_inputs(seed: int = 0) -> dict:
    splits = jax.random.split(jax.random.key(seed), 6)
    return {
        "frames": normal_values(splits[0], (VIDEOS, FRAME_TOK, D), 1.0, 6.0, ((0, 8), (1, 4))),
        "modulation": normal_values(splits[1], (VIDEOS, 2, D), 0.5, 3.0, ((0, 8),), jnp.float32),
        "w_qkv": normal_values(splits[2], (D, 3 * HEADS * HEAD_DIM), D ** -0.5, 0.109375, ((0, 8),)),
        "qk_gain": jnp.clip(1.0 + 0.18 * jax.random.normal(splits[3], (2, HEAD_DIM), jnp.float32), 0.1, 1.9),
        "w_out": normal_values(splits[4], (HEADS * HEAD_DIM, D), (HEADS * HEAD_DIM) ** -0.5, 0.375, ((1, 8),)),
    }


def norm_rows(frames_rows, modulation_rows):
    values_full = frames_rows.astype(jnp.float32)
    average = lax.optimization_barrier(jnp.mean(values_full, axis=-1, keepdims=True))
    centered = values_full - average
    spread = lax.optimization_barrier(jnp.mean(centered * centered, axis=-1, keepdims=True))
    normed = centered * lax.rsqrt(spread + 1e-06)
    return (normed * (1.0 + modulation_rows[0]) + modulation_rows[1]).astype(jnp.bfloat16)

def head_norm(projected, gain_row):
    count = projected.shape[0]
    shaped = projected.reshape(count, HEADS, HEAD_DIM)
    squares = lax.optimization_barrier(jnp.mean(shaped * shaped, axis=-1, keepdims=True))
    scaled = shaped * lax.rsqrt(squares + 1e-06) * gain_row
    return scaled.reshape(count, HEADS * HEAD_DIM).astype(jnp.bfloat16)

def reference(frames, modulation, w_qkv, qk_gain, w_out):
    width = HEADS * HEAD_DIM
    scale_factor = 1.0 / math.sqrt(HEAD_DIM)

    def attend_video(inputs):
        frames_video, modulation_video = inputs
        normed = norm_rows(frames_video, modulation_video)
        projected = jnp.dot(normed, w_qkv, preferred_element_type=jnp.float32)
        queries = head_norm(projected[:, :width], qk_gain[0])
        key_part = head_norm(projected[:, width:2 * width], qk_gain[1])
        value_part = projected[:, 2 * width:].astype(jnp.bfloat16)
        stacked = jnp.concatenate([key_part, value_part], axis=1)
        padded = jnp.pad(stacked, ((BORDER, BORDER), (0, 0)))

        def one_tile(tile_index):
            first_tile = tile_index - REACH
            query_tile = lax.dynamic_slice_in_dim(queries, (tile_index * TILE).astype(jnp.int32), TILE, 0)
            query_tile = query_tile.reshape(TILE, HEADS, HEAD_DIM).astype(jnp.float32)
            window = lax.dynamic_slice_in_dim(padded, (first_tile * TILE + BORDER).astype(jnp.int32), WINDOW, 0)
            positions = first_tile * TILE + jnp.arange(WINDOW, dtype=jnp.int32)
            inside = (positions >= 0) & (positions < FRAME_TOK)
            key_win = window[:, :width].reshape(WINDOW, HEADS, HEAD_DIM).astype(jnp.float32)
            value_win = window[:, width:].reshape(WINDOW, HEADS, HEAD_DIM).astype(jnp.float32)
            scores = jnp.einsum('qhd,khd->hqk', query_tile, key_win) * scale_factor
            raised = jnp.where(inside[None, None, :], jnp.exp(scores), 0.0)
            probs = (raised / lax.optimization_barrier(jnp.sum(raised, axis=-1, keepdims=True))).astype(jnp.bfloat16)
            return jnp.einsum('hqk,khd->qhd', probs.astype(jnp.float32), value_win).astype(jnp.bfloat16)
        attended = lax.map(one_tile, jnp.arange(TILES, dtype=jnp.int32)).reshape(FRAME_TOK, width)
        return jnp.dot(attended, w_out, preferred_element_type=jnp.float32).astype(jnp.bfloat16)
    return lax.map(attend_video, (frames, modulation))
```

```python
import functools
import math

import jax
import jax.numpy as jnp
from jax import lax
from jax.experimental import pallas as pl
from jax.experimental.pallas import tpu as pltpu
from jax.sharding import PartitionSpec as P

HEAD_DIM = 128
HEADS = 2
WIDTH = HEADS * HEAD_DIM
TILE = 128
REACH = 2
BORDER = REACH * TILE
VMEM_BYTES = 40 * 1024 * 1024

f32 = jnp.float32
bf16 = jnp.bfloat16
ANY = pl.BlockSpec(memory_space=pl.ANY)
VMEM = pl.BlockSpec(memory_space=pltpu.VMEM)


def params():
    return pltpu.CompilerParams(vmem_limit_bytes=VMEM_BYTES)


def dot(a, b):
    return jnp.dot(a, b, preferred_element_type=f32)


def dot_t(a, b):
    return lax.dot_general(a, b, (((1,), (1,)), ((), ())), preferred_element_type=f32)


def norm_kernel(frames_ref, modulation_ref, normed_ref):
    values = frames_ref[...].astype(f32)
    average = jnp.mean(values, axis=-1, keepdims=True)
    centered = values - average
    spread = jnp.mean(centered * centered, axis=-1, keepdims=True)
    normed = centered * lax.rsqrt(spread + 1e-06)
    normed_ref[...] = (normed * (1.0 + modulation_ref[0:1]) + modulation_ref[1:2]).astype(bf16)


def norm_rows(frames, modulation):
    rows, width = frames.shape
    block = TILE // 2
    return pl.pallas_call(
        norm_kernel,
        grid=(rows // block,),
        in_specs=[
            pl.BlockSpec((block, width), lambda i: (i, 0)),
            pl.BlockSpec((2, width), lambda i: (0, 0)),
        ],
        out_specs=pl.BlockSpec((block, width), lambda i: (i, 0)),
        out_shape=jax.ShapeDtypeStruct((rows, width), bf16),
        compiler_params=params(),
        cost_estimate=pl.CostEstimate(
            flops=10 * rows * width, bytes_accessed=4 * rows * width, transcendentals=rows
        ),
        name="layer_norm",
    )(frames, modulation)


def head_norm(projected, gain_row):
    parts = []
    for head in range(HEADS):
        x = projected[:, head * HEAD_DIM : (head + 1) * HEAD_DIM]
        squares = jnp.mean(x * x, axis=-1, keepdims=True)
        parts.append((x * lax.rsqrt(squares + 1e-06) * gain_row).astype(bf16))
    return parts


def project_kernel(plan, depth, normed_ref, gain_ref, *refs):
    count = len(plan.sources)
    sources = refs[:count]
    queries_ref, stacked_ref, weights, sems = refs[count:]
    copies = []
    groups = plan.groups()
    for first, pieces in groups:
        started = []
        for source, begin, rows, target in pieces:
            copy = pltpu.make_async_copy(
                sources[source].at[pl.ds(begin, rows)],
                weights.at[pl.ds(target, rows)],
                sems.at[sum(len(c) for c in copies) + len(started)],
            )
            copy.start()
            started.append(copy)
        copies.append(started)
    total = None
    for slot, (first, pieces) in enumerate(groups):
        for copy in copies[slot]:
            copy.wait()
        part = dot(
            normed_ref[:, pl.ds(first, depth)], weights[slot * depth : (slot + 1) * depth, :]
        )
        total = part if total is None else total + part
    for head, value in enumerate(head_norm(total[:, :WIDTH], gain_ref[0:1])):
        queries_ref[:, head * HEAD_DIM : (head + 1) * HEAD_DIM] = value
    for head, value in enumerate(head_norm(total[:, WIDTH : 2 * WIDTH], gain_ref[1:2])):
        stacked_ref[:, head * HEAD_DIM : (head + 1) * HEAD_DIM] = value
    stacked_ref[:, WIDTH:] = total[:, 2 * WIDTH :].astype(bf16)


def project(plan, normed, qk_gain):
    rows, width = normed.shape
    columns = plan.sources[0].shape[1]
    groups = len(plan.groups())
    pieces = sum(len(p) for _, p in plan.groups())
    return pl.pallas_call(
        functools.partial(project_kernel, plan, width // groups),
        in_specs=[VMEM, VMEM] + [ANY] * len(plan.sources),
        out_specs=[VMEM, VMEM],
        out_shape=[
            jax.ShapeDtypeStruct((rows, WIDTH), bf16),
            jax.ShapeDtypeStruct((rows, 2 * WIDTH), bf16),
        ],
        scratch_shapes=[
            pltpu.VMEM((width, columns), bf16),
            pltpu.SemaphoreType.DMA((pieces,)),
        ],
        compiler_params=params(),
        cost_estimate=pl.CostEstimate(
            flops=2 * rows * width * columns,
            bytes_accessed=2 * (rows * width + width * columns),
            transcendentals=rows,
        ),
        name="project",
    )(normed, qk_gain, *plan.sources)


def attend_kernel(
    out_plan, queries_ref, stacked_ref, before_ref, after_ref, *refs
):
    count = len(out_plan.sources)
    sources = refs[:count]
    mixed_ref, attended, blocks, sems = refs[count:]
    rows = queries_ref.shape[0]
    tiles = rows // TILE
    scale = 1.0 / math.sqrt(HEAD_DIM)
    place = lax.axis_index("frame")
    has_before = (place > 0).astype(f32)
    has_after = (place < lax.axis_size("frame") - 1).astype(f32)
    for head in range(HEADS):
        ks = slice(head * HEAD_DIM, (head + 1) * HEAD_DIM)
        vs = slice(WIDTH + head * HEAD_DIM, WIDTH + (head + 1) * HEAD_DIM)
        for tile in range(tiles):
            query = queries_ref[tile * TILE : (tile + 1) * TILE, ks]
            low, high = tile - REACH, tile + REACH + 1
            weighted = jnp.zeros((TILE, HEAD_DIM), f32)
            mass = jnp.zeros((TILE, 1), f32)
            spans = [(stacked_ref, max(low, 0), min(high, tiles), None)]
            if low < 0:
                spans.append((before_ref, low + REACH, REACH, has_before))
            if high > tiles:
                spans.append((after_ref, 0, high - tiles, has_after))
            for ref, begin, end, flag in spans:
                span = slice(begin * TILE, end * TILE)
                raised = jnp.exp(dot_t(query, ref[span, ks]) * scale)
                if flag is not None:
                    raised = raised * flag
                mass = mass + jnp.sum(raised, axis=-1, keepdims=True)
                weighted = weighted + dot(raised.astype(bf16), ref[span, vs])
            attended[tile * TILE : (tile + 1) * TILE, ks] = (weighted / mass).astype(bf16)
    width = blocks.shape[2]
    copies = []
    for source, begin, target in out_plan.blocks(width):
        number = len(copies)
        blocks[number] = dot(
            attended[...], sources[source][:, begin : begin + width]
        ).astype(bf16)
        copy = pltpu.make_async_copy(
            blocks.at[number],
            mixed_ref.at[0, :, pl.ds(pl.multiple_of(target, TILE), width)],
            sems.at[number],
        )
        copy.start()
        copies.append(copy)
    for copy in copies:
        copy.wait()


def attend(out_plan, queries, stacked, before, after, model, width):
    rows = queries.shape[0]
    return pl.pallas_call(
        functools.partial(attend_kernel, out_plan),
        in_specs=[VMEM] * (4 + len(out_plan.sources)),
        out_specs=ANY,
        out_shape=jax.ShapeDtypeStruct((1, rows, model), bf16),
        scratch_shapes=[
            pltpu.VMEM((rows, WIDTH), bf16),
            pltpu.VMEM((model // width, rows, width), bf16),
            pltpu.SemaphoreType.DMA((model // width,)),
        ],
        compiler_params=params(),
        cost_estimate=pl.CostEstimate(
            flops=2 * rows * WIDTH * (model + 2 * 5 * TILE),
            bytes_accessed=2 * (rows * model + WIDTH * model),
            transcendentals=rows * HEADS * 5 * TILE,
        ),
        name="attend_and_mix",
    )(queries, stacked, before, after, *out_plan.sources)


class WholeRows:
    def __init__(self, shard):
        self.sources = [lax.all_gather(shard, "fsdp", axis=0, tiled=True)]

    def groups(self):
        rows = self.sources[0].shape[0]
        return [(0, [(0, 0, rows, 0)])]


class WholeColumns:
    def __init__(self, shard):
        self.sources = [lax.all_gather(shard, "fsdp", axis=1, tiled=True)]

    def blocks(self, width):
        return [(0, i, i) for i in range(0, self.sources[0].shape[1], width)]


def swap(x, axis, bits):
    return lax.ppermute(x, axis, [(i, i ^ bits) for i in range(lax.axis_size(axis))])


def hop_order(chips):
    odd = [k for k in range(chips - 1, 0, -1) if k % 2]
    return odd + [k for k in range(2, chips, 2)]


class SplitRows:
    def __init__(self, shard):
        self.chips = lax.axis_size("fsdp") // 2
        self.shard_rows = shard.shape[0]
        half = self.shard_rows // 2
        quarter = half // 2
        place = lax.axis_index("frame")
        side = (place ^ (place >> 1)) & 1
        self.sources = [shard, swap(shard, "fsdp", 1)]
        self.hops = hop_order(self.chips)
        mine = lax.dynamic_slice_in_dim(shard, side * half, half, 0)
        come = {}
        for k in self.hops:
            come[k] = swap(mine, "fsdp", 2 * k) if k % 2 else swap(come[k + 1], "fsdp", 2)
        for k in self.hops:
            got = come[k]
            joined = jnp.concatenate(
                [got, swap(got[:quarter], "frame", 1), swap(got[quarter:], "frame", 2)], axis=0
            )
            self.sources += [joined, swap(joined, "fsdp", 1)]

    def groups(self):
        chip = lax.axis_index("fsdp") // 2
        core = lax.axis_index("fsdp") % 2
        place = lax.axis_index("frame")
        side = (place ^ (place >> 1)) & 1
        rows, half = self.shard_rows, self.shard_rows // 2

        def aligned(value):
            return pl.multiple_of(value, half)

        out = [
            (
                pl.multiple_of(chip * 2 * rows, 2 * rows),
                [(0, 0, rows, aligned(core * rows)), (1, 0, rows, aligned((1 - core) * rows))],
            )
        ]
        for slot, k in enumerate(self.hops, 1):
            pieces = []
            for source, half_core in ((2 * slot, core), (2 * slot + 1, 1 - core)):
                base = slot * 2 * rows + half_core * rows
                pieces.append((source, 0, half, aligned(base + side * half)))
                pieces.append((source, half, half, aligned(base + (1 - side) * half)))
            out.append((pl.multiple_of((chip ^ k) * 2 * rows, 2 * rows), pieces))
        return out


class SplitColumns:
    def __init__(self, shard):
        self.chips = lax.axis_size("fsdp") // 2
        self.sources = [shard, swap(shard, "fsdp", 1)]
        self.hops = hop_order(self.chips)
        come = {}
        for k in self.hops:
            come[k] = swap(shard, "fsdp", 2 * k) if k % 2 else swap(come[k + 1], "fsdp", 2)
            self.sources += [come[k], swap(come[k], "fsdp", 1)]

    def blocks(self, width):
        place = lax.axis_index("fsdp")
        out = []
        for slot, k in enumerate([0] + self.hops):
            for core in range(2):
                out.append((2 * slot + core, 0, (place ^ (2 * k + core)) * width))
        return out


def on_device(frames, modulation, w_qkv, qk_gain, w_out):
    devices, places = lax.axis_size("fsdp"), lax.axis_size("frame")
    chips = devices // 2
    split = (
        devices % 2 == 0
        and chips & (chips - 1) == 0
        and places % 4 == 0
        and w_qkv.shape[0] % TILE == 0
        and w_out.shape[1] % TILE == 0
    )
    model = frames.shape[2]
    rows_plan = (SplitRows if split else WholeRows)(w_qkv)
    normed = norm_rows(frames[0], modulation[0])
    queries, stacked = project(rows_plan, normed, qk_gain)
    ends = places - 1
    before = lax.ppermute(stacked[-BORDER:], "frame", [(i, i + 1) for i in range(ends)])
    after = lax.ppermute(stacked[:BORDER], "frame", [(i + 1, i) for i in range(ends)])
    columns_plan = (SplitColumns if split else WholeColumns)(w_out)
    width = w_out.shape[1] if split else 3 * TILE
    return attend(columns_plan, queries, stacked, before, after, model, width)


def solution(mesh):
    return jax.shard_map(
        on_device,
        mesh=mesh,
        in_specs=(
            P("fsdp", "frame", None),
            P("fsdp", None, None),
            P("fsdp", None),
            P(),
            P(None, "fsdp"),
        ),
        out_specs=P("fsdp", "frame", None),
        check_vma=False,
    )
```

```python
import functools
import math

import jax
import jax.numpy as jnp
from jax import lax
from jax.experimental import pallas as pl
from jax.experimental.pallas import tpu as pltpu
from jax.sharding import PartitionSpec as P

HEAD_DIM = 128
HEADS = 2
WIDTH = HEADS * HEAD_DIM
TILE = 128
REACH = 2
BORDER = REACH * TILE
VMEM_BYTES = 40 * 1024 * 1024

f32 = jnp.float32
bf16 = jnp.bfloat16
ANY = pl.BlockSpec(memory_space=pl.ANY)
VMEM = pl.BlockSpec(memory_space=pltpu.VMEM)


def params():
    return pltpu.CompilerParams(vmem_limit_bytes=VMEM_BYTES)


def dot(a, b):
    return jnp.dot(a, b, preferred_element_type=f32)


def dot_t(a, b):
    return lax.dot_general(a, b, (((1,), (1,)), ((), ())), preferred_element_type=f32)


def norm_kernel(frames_ref, modulation_ref, normed_ref, values_ref, rows_ref, sems):
    blocks, rows = values_ref.shape[0], values_ref.shape[1]
    copies = [pltpu.make_async_copy(modulation_ref, rows_ref, sems.at[blocks])]
    for i in range(blocks):
        copies.append(
            pltpu.make_async_copy(
                frames_ref.at[pl.ds(i * rows, rows)], values_ref.at[i], sems.at[i]
            )
        )
    for copy in copies:
        copy.start()
    copies[0].wait()
    scale, shift = 1.0 + rows_ref[0:1], rows_ref[1:2]
    for i in range(blocks):
        copies[1 + i].wait()
        values = values_ref[i].astype(f32)
        average = jnp.mean(values, axis=-1, keepdims=True)
        centered = values - average
        spread = jnp.mean(centered * centered, axis=-1, keepdims=True)
        normed = centered * lax.rsqrt(spread + 1e-06)
        normed_ref[i * rows : (i + 1) * rows] = (normed * scale + shift).astype(bf16)


def norm_rows(frames, modulation):
    rows, width = frames.shape
    block = TILE // 2
    return pl.pallas_call(
        norm_kernel,
        in_specs=[ANY, ANY],
        out_specs=VMEM,
        out_shape=jax.ShapeDtypeStruct((rows, width), bf16),
        scratch_shapes=[
            pltpu.VMEM((rows // block, block, width), bf16),
            pltpu.VMEM((2, width), f32),
            pltpu.SemaphoreType.DMA((rows // block + 1,)),
        ],
        compiler_params=params(),
        cost_estimate=pl.CostEstimate(
            flops=10 * rows * width, bytes_accessed=4 * rows * width, transcendentals=rows
        ),
        name="layer_norm",
    )(frames, modulation)


def head_norm(x, gain_row):
    squares = jnp.mean(x * x, axis=-1, keepdims=True)
    return (x * lax.rsqrt(squares + 1e-06) * gain_row).astype(bf16)


def project_kernel(count, starts, kinds, columns, resumed, gain_ref, *refs):
    lefts, rights = refs[:count], refs[count : 2 * count]
    total_ref, out_ref = refs[2 * count] if resumed else None, refs[-1]
    first, number = columns
    total = total_ref[:, first : first + number] if resumed else None
    for i in range(count):
        depth = rights[i].shape[0]
        left = lefts[i][...] if starts is None else lefts[i][:, pl.ds(starts()[i], depth)]
        part = dot(left, rights[i][:, first : first + number])
        total = part if total is None else total + part
    if kinds is None:
        out_ref[...] = total
        return
    for block, kind in enumerate(kinds):
        for head in range(HEADS):
            begin = block * WIDTH + head * HEAD_DIM
            x = total[:, begin : begin + HEAD_DIM]
            out_ref[:, begin : begin + HEAD_DIM] = (
                x.astype(bf16) if kind is None else head_norm(x, gain_ref[kind : kind + 1])
            )


def project(pairs, qk_gain, columns, name, starts=None, kinds=None, total=None):
    lefts, rights = [list(side) for side in zip(*pairs)]
    rows = lefts[0].shape[0]
    depth = sum(right.shape[0] for right in rights)
    resumed = total is not None
    operands = [qk_gain, *lefts, *rights] + [total] * resumed
    return pl.pallas_call(
        functools.partial(project_kernel, len(pairs), starts, kinds, columns, resumed),
        in_specs=[VMEM] * len(operands),
        out_specs=VMEM,
        out_shape=jax.ShapeDtypeStruct((rows, columns[1]), f32 if kinds is None else bf16),
        compiler_params=params(),
        cost_estimate=pl.CostEstimate(
            flops=2 * rows * depth * columns[1],
            bytes_accessed=2 * depth * (rows + columns[1]),
            transcendentals=rows,
        ),
        name=name,
    )(*operands)


def arrange_kernel(starts, order, homes, normed_ref, *out_refs):
    rows = normed_ref.shape[0]
    places, cores = starts()
    depth = normed_ref.shape[1] // lax.axis_size("fsdp")
    quarter = depth // 4
    source = lax.broadcasted_iota(jnp.int32, (depth, depth), 0)
    target = lax.broadcasted_iota(jnp.int32, (depth, depth), 1)
    for here in range(2):
        wanted = target
        for i, number in enumerate(order(cores[here])):
            inside = (target >= i * quarter) & (target < (i + 1) * quarter)
            wanted = jnp.where(inside, target + (number - i) * quarter, wanted)
        chosen = (source == wanted).astype(f32).astype(bf16)
        for slot, place in enumerate(places[here]):
            strip = normed_ref[:, pl.ds(pl.multiple_of(place, TILE), depth)]
            moved = dot(strip, chosen).astype(bf16)
            for i, (out, at) in enumerate(homes[slot]):
                out_refs[2 * out + here][:, at * quarter : (at + 1) * quarter] = moved[
                    :, i * quarter : (i + 1) * quarter
                ]


def arrange(starts, order, homes, widths, normed):
    rows = normed.shape[0]
    shapes = [jax.ShapeDtypeStruct((rows, width), bf16) for width in widths for _ in range(2)]
    return pl.pallas_call(
        functools.partial(arrange_kernel, starts, order, homes),
        in_specs=[VMEM],
        out_specs=[VMEM] * len(shapes),
        out_shape=shapes,
        compiler_params=params(),
        cost_estimate=pl.CostEstimate(
            flops=8 * rows * normed.shape[1] * TILE, bytes_accessed=4 * rows * normed.shape[1],
            transcendentals=0,
        ),
        name="arrange",
    )(normed)


def load(sources, pieces, weights, sems):
    started = []
    for source, column in pieces:
        copy = pltpu.make_async_copy(
            sources[source],
            weights.at[:, pl.ds(column, sources[source].shape[1])],
            sems.at[len(started)],
        )
        copy.start()
        started.append(copy)
    return started


def attend_kernel(layout, count, queries_ref, stacked_ref, before_ref, after_ref, *refs):
    sources = refs[:count]
    mixed_ref, attended, weights, blocks, sems, out_sems = refs[count:]
    copies = load(sources, layout(), weights, sems)
    rows = queries_ref.shape[0]
    tiles = rows // TILE
    scale = 1.0 / math.sqrt(HEAD_DIM)
    place = lax.axis_index("frame")
    has_before = (place > 0).astype(f32)
    has_after = (place < lax.axis_size("frame") - 1).astype(f32)
    for head in range(HEADS):
        ks = slice(head * HEAD_DIM, (head + 1) * HEAD_DIM)
        vs = slice(WIDTH + head * HEAD_DIM, WIDTH + (head + 1) * HEAD_DIM)
        for tile in range(tiles):
            query = queries_ref[tile * TILE : (tile + 1) * TILE, ks]
            low, high = tile - REACH, tile + REACH + 1
            weighted = jnp.zeros((TILE, HEAD_DIM), f32)
            mass = jnp.zeros((TILE, 1), f32)
            spans = [(stacked_ref, max(low, 0), min(high, tiles), None)]
            if low < 0:
                spans.append((before_ref, low + REACH, REACH, has_before))
            if high > tiles:
                spans.append((after_ref, 0, high - tiles, has_after))
            for ref, begin, end, flag in spans:
                span = slice(begin * TILE, end * TILE)
                keys, values = ref[span, ks], ref[span, vs]
                raised = jnp.exp(dot_t(query, keys) * scale)
                if flag is not None:
                    raised = raised * flag
                mass = mass + jnp.sum(raised, axis=-1, keepdims=True)
                weighted = weighted + dot(raised.astype(bf16), values)
            attended[tile * TILE : (tile + 1) * TILE, ks] = (weighted / mass).astype(bf16)
    for copy in copies:
        copy.wait()
    number, width = blocks.shape[0], blocks.shape[2]
    copies = []
    for block in range(number):
        columns = slice(block * width, (block + 1) * width)
        blocks[block] = dot(attended[...], weights[:, columns]).astype(bf16)
        copy = pltpu.make_async_copy(
            blocks.at[block], mixed_ref.at[0, :, columns], out_sems.at[block]
        )
        copy.start()
        copies.append(copy)
    for copy in copies:
        copy.wait()


def attend(layout, sources, queries, stacked, before, after, model):
    rows = queries.shape[0]
    width = 4 * TILE if model % (4 * TILE) == 0 else TILE
    return pl.pallas_call(
        functools.partial(attend_kernel, layout, len(sources)),
        in_specs=[VMEM] * 4 + [ANY] * len(sources),
        out_specs=ANY,
        out_shape=jax.ShapeDtypeStruct((1, rows, model), bf16),
        scratch_shapes=[
            pltpu.VMEM((rows, WIDTH), bf16),
            pltpu.VMEM((WIDTH, model), bf16),
            pltpu.VMEM((model // width, rows, width), bf16),
            pltpu.SemaphoreType.DMA((len(layout()),)),
            pltpu.SemaphoreType.DMA((model // width,)),
        ],
        compiler_params=params(),
        cost_estimate=pl.CostEstimate(
            flops=2 * rows * WIDTH * (model + 2 * 5 * TILE),
            bytes_accessed=2 * (rows * model + WIDTH * model),
            transcendentals=rows * HEADS * 5 * TILE,
        ),
        name="attend_and_mix",
    )(queries, stacked, before, after, *sources)


def swap(x, axis, bits):
    return lax.ppermute(x, axis, [(i, i ^ bits) for i in range(lax.axis_size(axis))])


def swap_plane(x, turn):
    places = lax.axis_size("frame")
    pairs = []
    for i in range(lax.axis_size("fsdp")):
        for j in range(places):
            pairs.append((i * places + j, i * places + (j ^ (1 + (i + turn) % 2))))
    return lax.ppermute(x, ("fsdp", "frame"), pairs)


def hop_order(chips):
    odd = [k for k in range(chips - 1, 0, -1) if k % 2]
    return odd + [k for k in range(2, chips, 2)]


def split_plan(frames, modulation, w_qkv, w_out, qk_gain):
    chips = lax.axis_size("fsdp") // 2
    shard_rows, columns = w_qkv.shape
    shard_columns = w_out.shape[1]
    quarter = shard_rows // 4
    hops = hop_order(chips)
    odd, even = [k for k in hops if k % 2], [k for k in hops if k % 2 == 0]
    far = [k for k in hops if k != 1]
    ring = [1] + far
    fence = lax.optimization_barrier

    def where():
        place, index = lax.axis_index("frame"), lax.axis_index("fsdp")
        high = (place >> 1) & 1
        return index // 2, index % 2, 2 * ((place & 1) ^ high) + high

    def order(core):
        spot = where()[2]
        return spot, spot ^ (2 + core), spot ^ (3 - core), spot ^ 1

    def shard_places():
        chip, core, _ = where()
        cores = (core, 1 - core)
        return [[((chip ^ k) * 2 + c) * shard_rows for k in ring] for c in cores], cores

    def own_places():
        chip, core, _ = where()
        return [pl.multiple_of((2 * chip + c) * shard_rows, TILE) for c in (core, 1 - core)]

    def out_layout():
        chip, core, _ = where()
        place = 2 * chip + core
        pieces = []
        for slot, k in enumerate([0] + hops):
            for source, here in ((2 * slot, 2 * k), (2 * slot + 1, 2 * k + 1)):
                pieces.append((source, pl.multiple_of((place ^ here) * shard_columns, TILE)))
        return pieces

    spot = where()[2]
    part = lax.dynamic_slice_in_dim(w_qkv, spot * quarter, quarter, 0)
    come = {k: swap(part, "fsdp", 2 * k) for k in odd}
    other_qkv = swap(w_qkv, "fsdp", 1)
    other_out = swap(w_out, "fsdp", 1)
    normed = norm_rows(frames, modulation)
    normed, *got = fence((normed, *[come[k] for k in odd if k != 1]))
    come.update(zip([k for k in odd if k != 1], got))

    for k in even:
        come[k] = swap(come[k + 1], "fsdp", 2)
    total = project(
        [(normed, w_qkv), (normed, other_qkv)], qk_gain, (0, columns), "project_own", own_places
    )
    rest_part = lax.dynamic_slice_in_dim(w_qkv, (spot ^ 1) * quarter, quarter, 0)
    total, rest_part, *got = fence((total, rest_part, *[come[k] for k in [1] + even]))
    come.update(zip([1] + even, got))

    count = len(ring)
    first = jnp.concatenate([come[k] for k in ring], axis=0)
    first_rest = swap_plane(first, 0)
    across = swap(rest_part, "fsdp", 2)
    first_other = swap(first, "fsdp", 1)
    homes = [
        [(0, slot), (1, slot), (2, slot), (2, count + slot - 1) if slot else (3, 0)]
        for slot in range(count)
    ]
    widths = [count * quarter, count * quarter, (2 * count - 1) * quarter, quarter]
    arranged = arrange(shard_places, order, homes, widths, normed)
    first, first_rest, across, first_other, arranged = fence(
        (first, first_rest, across, first_other, arranged)
    )

    second = jnp.concatenate([first, first_rest[quarter:]], axis=0)
    second_rest = swap_plane(second, 1)
    outs = {k: swap(w_out, "fsdp", 2 * k) for k in odd}
    first_rest_other = swap(first_rest, "fsdp", 1)
    across_other = swap(across, "fsdp", 1)
    pieces = [first, first_other, first_rest, first_rest_other, across, across_other]
    lefts = [arranged[i] for i in (0, 1, 2, 3, 6, 7)]
    total = project(list(zip(lefts, pieces)), qk_gain, (0, columns), "project_mid", total=total)
    total, second_rest, *got = fence((total, second_rest, *[outs[k] for k in odd]))
    outs.update(zip(odd, got))

    second_rest_other = swap(second_rest, "fsdp", 1)
    last = [(arranged[4], second_rest), (arranged[5], second_rest_other)]
    stacked = project(
        last, qk_gain, (WIDTH, 2 * WIDTH), "project_keys_values", kinds=(1, None), total=total
    )
    queries = project(last, qk_gain, (0, WIDTH), "project_queries", kinds=(0,), total=total)
    for k in even:
        outs[k] = swap(outs[k + 1], "fsdp", 2)
    sources = [w_out, other_out]
    for k in hops:
        sources += [outs[k], swap(outs[k], "fsdp", 1)]
    return queries, stacked, out_layout, sources


def whole_plan(frames, modulation, w_qkv, w_out, qk_gain):
    rows = lax.all_gather(w_qkv, "fsdp", axis=0, tiled=True)
    columns = lax.all_gather(w_out, "fsdp", axis=1, tiled=True)
    normed = norm_rows(frames, modulation)
    stacked = project(
        [(normed, rows)], qk_gain, (WIDTH, 2 * WIDTH), "project_keys_values", kinds=(1, None)
    )
    queries = project([(normed, rows)], qk_gain, (0, WIDTH), "project_queries", kinds=(0,))
    return queries, stacked, lambda: [(0, 0)], [columns]


def on_device(frames, modulation, w_qkv, qk_gain, w_out):
    devices, places = lax.axis_size("fsdp"), lax.axis_size("frame")
    chips = devices // 2
    split = (
        devices % 2 == 0
        and chips > 1
        and chips & (chips - 1) == 0
        and places % 4 == 0
        and w_qkv.shape[0] % TILE == 0
        and w_out.shape[1] % TILE == 0
    )
    plan = split_plan if split else whole_plan
    queries, stacked, layout, sources = plan(frames[0], modulation[0], w_qkv, w_out, qk_gain)
    ends = places - 1
    before = lax.ppermute(stacked[-BORDER:], "frame", [(i, i + 1) for i in range(ends)])
    behind = lax.ppermute(stacked[:BORDER], "frame", [(i + 1, i) for i in range(ends)])
    return attend(layout, sources, queries, stacked, before, behind, frames.shape[2])


def solution(mesh):
    return jax.shard_map(
        on_device,
        mesh=mesh,
        in_specs=(
            P("fsdp", "frame", None),
            P("fsdp", None, None),
            P("fsdp", None),
            P(),
            P(None, "fsdp"),
        ),
        out_specs=P("fsdp", "frame", None),
        check_vma=False,
    )
```

```python
import functools
import math

import jax
import jax.numpy as jnp
from jax import lax
from jax.experimental import pallas as pl
from jax.experimental.pallas import tpu as pltpu
from jax.sharding import PartitionSpec as P

HEAD_DIM = 128
HEADS = 2
WIDTH = HEADS * HEAD_DIM
TILE = 128
REACH = 2
BORDER = REACH * TILE
VMEM_BYTES = 40 * 1024 * 1024

f32 = jnp.float32
bf16 = jnp.bfloat16
ANY = pl.BlockSpec(memory_space=pl.ANY)
VMEM = pl.BlockSpec(memory_space=pltpu.VMEM)


def params():
    return pltpu.CompilerParams(vmem_limit_bytes=VMEM_BYTES)


def dot(a, b):
    return jnp.dot(a, b, preferred_element_type=f32)


def dot_t(a, b):
    return lax.dot_general(a, b, (((1,), (1,)), ((), ())), preferred_element_type=f32)


def norm_kernel(frames_ref, modulation_ref, normed_ref):
    values = frames_ref[...].astype(f32)
    average = jnp.mean(values, axis=-1, keepdims=True)
    centered = values - average
    spread = jnp.mean(centered * centered, axis=-1, keepdims=True)
    normed = centered * lax.rsqrt(spread + 1e-06)
    normed_ref[...] = (normed * (1.0 + modulation_ref[0:1]) + modulation_ref[1:2]).astype(bf16)


def norm_rows(frames, modulation):
    rows, width = frames.shape
    block = TILE // 2
    return pl.pallas_call(
        norm_kernel,
        grid=(rows // block,),
        in_specs=[
            pl.BlockSpec((block, width), lambda i: (i, 0)),
            pl.BlockSpec((2, width), lambda i: (0, 0)),
        ],
        out_specs=pl.BlockSpec((block, width), lambda i: (i, 0)),
        out_shape=jax.ShapeDtypeStruct((rows, width), bf16),
        compiler_params=params(),
        cost_estimate=pl.CostEstimate(
            flops=10 * rows * width, bytes_accessed=4 * rows * width, transcendentals=rows
        ),
        name="layer_norm",
    )(frames, modulation)


def head_norm(x, gain_row):
    squares = jnp.mean(x * x, axis=-1, keepdims=True)
    return (x * lax.rsqrt(squares + 1e-06) * gain_row).astype(bf16)


def project_kernel(count, starts, kinds, columns, resumed, gain_ref, *refs):
    lefts, rights = refs[:count], refs[count : 2 * count]
    total_ref, refs = refs[2 * count] if resumed else None, refs[2 * count + resumed :]
    out_ref = refs[0]
    first, number = columns
    total = total_ref[:, first : first + number] if resumed else None
    for i in range(count):
        depth = rights[i].shape[0]
        left = lefts[i][...] if starts is None else lefts[i][:, pl.ds(starts()[i], depth)]
        part = dot(left, rights[i][:, first : first + number])
        total = part if total is None else total + part
    if kinds is None:
        out_ref[...] = total
        return
    for block, kind in enumerate(kinds):
        for head in range(HEADS):
            begin = block * WIDTH + head * HEAD_DIM
            x = total[:, begin : begin + HEAD_DIM]
            out_ref[:, begin : begin + HEAD_DIM] = (
                x.astype(bf16) if kind is None else head_norm(x, gain_ref[kind : kind + 1])
            )


def project(pairs, qk_gain, columns, name, starts=None, kinds=None, total=None):
    lefts, rights = [list(side) for side in zip(*pairs)]
    rows = lefts[0].shape[0]
    depth = sum(right.shape[0] for right in rights)
    resumed = total is not None
    operands = [qk_gain, *lefts, *rights] + [total] * resumed
    return pl.pallas_call(
        functools.partial(project_kernel, len(pairs), starts, kinds, columns, resumed),
        in_specs=[VMEM] * len(operands),
        out_specs=VMEM,
        out_shape=jax.ShapeDtypeStruct((rows, columns[1]), f32 if kinds is None else bf16),
        compiler_params=params(),
        cost_estimate=pl.CostEstimate(
            flops=2 * rows * depth * columns[1],
            bytes_accessed=2 * depth * (rows + columns[1]),
            transcendentals=rows,
        ),
        name=name,
    )(*operands)


def arrange_kernel(starts, order, homes, normed_ref, *out_refs):
    rows = normed_ref.shape[0]
    places, cores = starts()
    depth = normed_ref.shape[1] // lax.axis_size("fsdp")
    quarter = depth // 4
    source = lax.broadcasted_iota(jnp.int32, (depth, depth), 0)
    target = lax.broadcasted_iota(jnp.int32, (depth, depth), 1)
    for here in range(2):
        wanted = target
        for i, number in enumerate(order(cores[here])):
            inside = (target >= i * quarter) & (target < (i + 1) * quarter)
            wanted = jnp.where(inside, target + (number - i) * quarter, wanted)
        chosen = (source == wanted).astype(f32).astype(bf16)
        for slot, place in enumerate(places[here]):
            strip = normed_ref[:, pl.ds(pl.multiple_of(place, TILE), depth)]
            moved = dot(strip, chosen).astype(bf16)
            for i, (out, at) in enumerate(homes[slot]):
                out_refs[2 * out + here][:, at * quarter : (at + 1) * quarter] = moved[
                    :, i * quarter : (i + 1) * quarter
                ]


def arrange(starts, order, homes, widths, normed):
    rows = normed.shape[0]
    shapes = [jax.ShapeDtypeStruct((rows, width), bf16) for width in widths for _ in range(2)]
    return pl.pallas_call(
        functools.partial(arrange_kernel, starts, order, homes),
        in_specs=[VMEM],
        out_specs=[VMEM] * len(shapes),
        out_shape=shapes,
        compiler_params=params(),
        cost_estimate=pl.CostEstimate(
            flops=8 * rows * normed.shape[1] * TILE, bytes_accessed=4 * rows * normed.shape[1],
            transcendentals=0,
        ),
        name="arrange",
    )(normed)


def load(sources, pieces, weights, sems):
    started = []
    for source, row, columns, place in pieces:
        copy = pltpu.make_async_copy(
            sources[source].at[pl.ds(row, weights.shape[0])],
            weights.at[:, pl.ds(pl.multiple_of(place, TILE), columns)],
            sems.at[len(started)],
        )
        copy.start()
        started.append(copy)
    return started


def heads():
    for head in range(HEADS):
        ks = slice(head * HEAD_DIM, (head + 1) * HEAD_DIM)
        yield ks, slice(WIDTH + head * HEAD_DIM, WIDTH + (head + 1) * HEAD_DIM)


def share(query, keys, values, flag=None):
    raised = jnp.exp(dot_t(query, keys) * (1.0 / math.sqrt(HEAD_DIM)))
    if flag is not None:
        raised = raised * flag
    return dot(raised.astype(bf16), values), jnp.sum(raised, axis=-1, keepdims=True)


def attend_own_kernel(queries_ref, stacked_ref, weighted_ref, mass_ref):
    tiles = queries_ref.shape[0] // TILE
    for ks, vs in heads():
        for tile in range(tiles):
            rows = slice(tile * TILE, (tile + 1) * TILE)
            span = slice(max(tile - REACH, 0) * TILE, min(tile + REACH + 1, tiles) * TILE)
            weighted, mass = share(queries_ref[rows, ks], stacked_ref[span, ks], stacked_ref[span, vs])
            weighted_ref[rows, ks] = weighted
            mass_ref[rows, ks] = jnp.broadcast_to(mass, (TILE, HEAD_DIM))


def attend_own(queries, stacked):
    rows = queries.shape[0]
    return pl.pallas_call(
        attend_own_kernel,
        in_specs=[VMEM] * 2,
        out_specs=[VMEM] * 2,
        out_shape=[jax.ShapeDtypeStruct((rows, WIDTH), f32)] * 2,
        compiler_params=params(),
        cost_estimate=pl.CostEstimate(
            flops=4 * rows * rows * WIDTH, bytes_accessed=14 * rows * WIDTH,
            transcendentals=rows * rows * HEADS,
        ),
        name="attend_own_slab",
    )(queries, stacked)


def attend_kernel(layout, count, arrivals, queries_ref, weighted_ref, mass_ref, *refs):
    near_ref, arrived, refs = refs[0], refs[1:arrivals], refs[arrivals:]
    sources = refs[:count]
    mixed_ref, before, behind, attended, weights, blocks, sems, out_sems = refs[count:]
    copies = load(sources, layout(), weights, sems)
    tiles = queries_ref.shape[0] // TILE
    place = lax.axis_index("frame")
    far = arrived[0][...]
    for ref in arrived[1:]:
        far = far + ref[...]
    odd = (place & 1) == 1
    before[...] = jnp.where(odd, near_ref[...], far)
    behind[...] = jnp.where(odd, far, near_ref[...])
    has_before = (place > 0).astype(f32)
    has_behind = (place < lax.axis_size("frame") - 1).astype(f32)
    for ks, vs in heads():
        for tile in range(tiles):
            rows = slice(tile * TILE, (tile + 1) * TILE)
            weighted, mass = weighted_ref[rows, ks], mass_ref[rows, ks]
            low, high = tile - REACH, tile + REACH + 1 - tiles
            spans = []
            if low < 0:
                spans.append((before, slice((low + REACH) * TILE, BORDER), has_before))
            if high > 0:
                spans.append((behind, slice(0, high * TILE), has_behind))
            for ref, span, flag in spans:
                more, extra = share(queries_ref[rows, ks], ref[span, ks], ref[span, vs], flag)
                weighted, mass = weighted + more, mass + extra
            attended[rows, ks] = (weighted / mass).astype(bf16)
    for copy in copies:
        copy.wait()
    number, width = blocks.shape[0], blocks.shape[2]
    copies = []
    for block in range(number):
        columns = slice(block * width, (block + 1) * width)
        blocks[block] = dot(attended[...], weights[:, columns]).astype(bf16)
        copy = pltpu.make_async_copy(
            blocks.at[block], mixed_ref.at[0, :, columns], out_sems.at[block]
        )
        copy.start()
        copies.append(copy)
    for copy in copies:
        copy.wait()


def attend(layout, sources, queries, own, edges, model):
    rows = queries.shape[0]
    width = 4 * TILE if model % (4 * TILE) == 0 else TILE
    return pl.pallas_call(
        functools.partial(attend_kernel, layout, len(sources), len(edges)),
        in_specs=[VMEM] * (3 + len(edges)) + [ANY] * len(sources),
        out_specs=ANY,
        out_shape=jax.ShapeDtypeStruct((1, rows, model), bf16),
        scratch_shapes=[
            pltpu.VMEM((BORDER, 2 * WIDTH), bf16),
            pltpu.VMEM((BORDER, 2 * WIDTH), bf16),
            pltpu.VMEM((rows, WIDTH), bf16),
            pltpu.VMEM((WIDTH, model), bf16),
            pltpu.VMEM((model // width, rows, width), bf16),
            pltpu.SemaphoreType.DMA((len(layout()),)),
            pltpu.SemaphoreType.DMA((model // width,)),
        ],
        compiler_params=params(),
        cost_estimate=pl.CostEstimate(
            flops=2 * rows * WIDTH * (model + 4 * TILE),
            bytes_accessed=2 * (rows * model + WIDTH * model),
            transcendentals=rows * HEADS * 2 * TILE,
        ),
        name="attend_and_mix",
    )(queries, *own, *edges, *sources)


def swap(x, axis, bits):
    return lax.ppermute(x, axis, [(i, i ^ bits) for i in range(lax.axis_size(axis))])


def swap_plane(x, turn):
    places = lax.axis_size("frame")
    pairs = []
    for i in range(lax.axis_size("fsdp")):
        for j in range(places):
            pairs.append((i * places + j, i * places + (j ^ (1 + (i + turn) % 2))))
    return lax.ppermute(x, ("fsdp", "frame"), pairs)


def hop_order(chips):
    odd = [k for k in range(chips - 1, 0, -1) if k % 2]
    return odd + [k - 1 for k in odd if k > 1]


def halos(stacked):
    places = lax.axis_size("frame")
    odd = lax.axis_index("frame") & 1
    tail = stacked.shape[0] - BORDER
    near = lax.dynamic_slice_in_dim(stacked, (1 - odd) * tail, BORDER, 0)
    far = lax.dynamic_slice_in_dim(stacked, odd * tail, BORDER, 0)
    straight, out, on = [], [], []
    for i in range(lax.axis_size("fsdp")):
        for j in range(0, places, 4):
            for source, way, target in ((1, 3, 2), (2, 0, 1)):
                place = i * places + j
                if i % 2:
                    out.append((place + source, place + way))
                    on.append((place + way, place + target))
                else:
                    straight.append((place + source, place + target))
    axes = ("fsdp", "frame")
    way = lax.ppermute(far, axes, out)
    arrived = [lax.ppermute(way, axes, on), lax.ppermute(far, axes, straight)]
    if places > 4:
        pairs = [(j, j + 1) for j in range(3, places - 1, 4)]
        arrived.append(lax.ppermute(far, "frame", pairs + [(b, a) for a, b in pairs]))
    return [swap(near, "frame", 1)] + arrived


def split_plan(frames, modulation, w_qkv, w_out, qk_gain):
    chips = lax.axis_size("fsdp") // 2
    shard_rows, columns = w_qkv.shape
    shard_columns = w_out.shape[1]
    quarter = shard_rows // 4
    hops = hop_order(chips)
    odd, even = [k for k in hops if k % 2], [k for k in hops if k % 2 == 0]
    front, back = [k for k in odd if k > 1], even
    ring = [1] + front + back
    fence = lax.optimization_barrier

    def where():
        place, index = lax.axis_index("frame"), lax.axis_index("fsdp")
        high = (place >> 1) & 1
        return index // 2, index % 2, 2 * ((place & 1) ^ high) + high

    def order(core):
        spot = where()[2]
        return spot, spot ^ (2 + core), spot ^ (3 - core), spot ^ 1

    def shard_places():
        chip, core, _ = where()
        cores = (core, 1 - core)
        return [[((chip ^ k) * 2 + c) * shard_rows for k in ring] for c in cores], cores

    def own_places():
        chip, core, _ = where()
        return [pl.multiple_of((2 * chip + c) * shard_rows, TILE) for c in (core, 1 - core)]

    def out_layout():
        chip, core, _ = where()
        place = 2 * chip + core
        return [
            (source, 0, shard_columns, (place ^ (2 * k + here)) * shard_columns)
            for source, (k, here) in enumerate((k, here) for k in [0] + ring for here in (0, 1))
        ]

    spot = where()[2]
    part = lax.dynamic_slice_in_dim(w_qkv, spot * quarter, quarter, 0)
    come = [swap(part, "fsdp", 2 * k) for k in front]
    near = swap(part, "fsdp", 2)
    other_qkv = swap(w_qkv, "fsdp", 1)
    other_out = swap(w_out, "fsdp", 1)
    normed = norm_rows(frames, modulation)
    normed, come = fence((normed, come))

    late = [swap(x, "fsdp", 2) for x in come]
    one = jnp.concatenate(come, axis=0)
    one_rest = swap_plane(one, 0)
    total = project(
        [(normed, w_qkv), (normed, other_qkv)], qk_gain, (0, columns), "project_own", own_places
    )
    nf, nb = len(front), len(back)
    homes = [[(4, nb), (5, 2 * nb), (2, 2 * nf + nb), (3, 0)]]
    homes += [[(0, i), (1, i), (2, i), (2, nf + i)] for i in range(nf)]
    homes += [[(4, i), (5, i), (2, 2 * nf + i), (5, nb + i)] for i in range(nb)]
    widths = [quarter * n for n in (nf, nf, 2 * nf + nb + 1, 1, nb + 1, 2 * nb + 1)]
    arranged = arrange(shard_places, order, homes, widths, normed)
    next_part = lax.dynamic_slice_in_dim(w_qkv, (spot ^ 1) * quarter, quarter, 0)
    one, one_rest, late, near, total, arranged, next_part = fence(
        (one, one_rest, late, near, total, arranged, next_part)
    )

    late = jnp.concatenate(late + [near], axis=0)
    two = swap_plane(jnp.concatenate([one, one_rest, late], axis=0), 1)
    across = swap(next_part, "fsdp", 2)
    cut = 2 * (shard_columns // TILE) // 3 * TILE
    wides = [swap(w_out[:, :cut], "fsdp", 2 * k) for k in front]
    one_other, one_rest_other = swap(one, "fsdp", 1), swap(one_rest, "fsdp", 1)
    late_other = swap(late, "fsdp", 1)
    two, across, late, one_other, one_rest_other, late_other, wides = fence(
        (two, across, late, one_other, one_rest_other, late_other, wides)
    )

    relayed = two[2 * nf * quarter : (2 * nf + nb) * quarter]
    three = swap_plane(
        jnp.concatenate([late[: nb * quarter], relayed, late[nb * quarter :]], axis=0), 0
    )
    narrows = [swap(w_out[:, cut:], "fsdp", 2 * k) for k in front]
    pieces = [one, one_other, one_rest, one_rest_other, two, swap(two, "fsdp", 1)]
    pieces += [across, swap(across, "fsdp", 1), late, late_other]
    total = project(
        list(zip(arranged[:10], pieces)), qk_gain, (0, columns), "project_mid", total=total
    )
    total, three, narrows = fence((total, three, narrows))

    last = [(arranged[10], three), (arranged[11], swap(three, "fsdp", 1))]
    stacked = project(
        last, qk_gain, (WIDTH, 2 * WIDTH), "project_keys_values", kinds=(1, None), total=total
    )
    queries = project(last, qk_gain, (0, WIDTH), "project_queries", kinds=(0,), total=total)

    joined = [jnp.concatenate(pair, axis=1) for pair in zip(wides, narrows)]
    sources = [w_out, other_out]
    edges = halos(stacked)
    for x in [swap(w_out, "fsdp", 2)] + joined + [swap(x, "fsdp", 2) for x in joined]:
        sources += [x, swap(fence((x, edges[0]))[0], "fsdp", 1)]
    return queries, stacked, edges, out_layout, sources


def whole_plan(frames, modulation, w_qkv, w_out, qk_gain):
    rows = lax.all_gather(w_qkv, "fsdp", axis=0, tiled=True)
    columns = lax.all_gather(w_out, "fsdp", axis=1, tiled=True)
    normed = norm_rows(frames, modulation)
    stacked = project(
        [(normed, rows)], qk_gain, (WIDTH, 2 * WIDTH), "project_keys_values", kinds=(1, None)
    )
    queries = project([(normed, rows)], qk_gain, (0, WIDTH), "project_queries", kinds=(0,))
    return queries, stacked, halos(stacked), lambda: [(0, 0, columns.shape[1], 0)], [columns]


def on_device(frames, modulation, w_qkv, qk_gain, w_out):
    devices, places = lax.axis_size("fsdp"), lax.axis_size("frame")
    chips = devices // 2
    split = (
        devices % 2 == 0
        and chips > 2
        and chips & (chips - 1) == 0
        and w_qkv.shape[0] % TILE == 0
        and w_out.shape[1] % TILE == 0
    )
    plan = split_plan if split else whole_plan
    queries, stacked, edges, layout, sources = plan(
        frames[0], modulation[0], w_qkv, w_out, qk_gain
    )
    own = attend_own(queries, stacked)
    return attend(layout, sources, queries, own, edges, frames.shape[2])


def solution(mesh):
    return jax.shard_map(
        on_device,
        mesh=mesh,
        in_specs=(
            P("fsdp", "frame", None),
            P("fsdp", None, None),
            P("fsdp", None),
            P(),
            P(None, "fsdp"),
        ),
        out_specs=P("fsdp", "frame", None),
        check_vma=False,
    )
```

```python
import functools
import math

import jax
import jax.numpy as jnp
from jax import lax
from jax.experimental import pallas as pl
from jax.experimental.pallas import tpu as pltpu
from jax.sharding import PartitionSpec as P

HEAD_DIM = 128
HEADS = 2
WIDTH = HEADS * HEAD_DIM
TILE = 128
REACH = 2
BORDER = REACH * TILE
VMEM_BYTES = 40 * 1024 * 1024

f32 = jnp.float32
bf16 = jnp.bfloat16
ANY = pl.BlockSpec(memory_space=pl.ANY)
VMEM = pl.BlockSpec(memory_space=pltpu.VMEM)


def params():
    return pltpu.CompilerParams(vmem_limit_bytes=VMEM_BYTES)


def dot(a, b):
    return jnp.dot(a, b, preferred_element_type=f32)


def dot_t(a, b):
    return lax.dot_general(a, b, (((1,), (1,)), ((), ())), preferred_element_type=f32)


def norm_kernel(frames_ref, modulation_ref, normed_ref):
    values = frames_ref[...].astype(f32)
    average = jnp.mean(values, axis=-1, keepdims=True)
    centered = values - average
    spread = jnp.mean(centered * centered, axis=-1, keepdims=True)
    normed = centered * lax.rsqrt(spread + 1e-06)
    normed_ref[...] = (normed * (1.0 + modulation_ref[0:1]) + modulation_ref[1:2]).astype(bf16)


def norm_rows(frames, modulation):
    rows, width = frames.shape
    block = TILE // 2
    return pl.pallas_call(
        norm_kernel,
        grid=(rows // block,),
        in_specs=[
            pl.BlockSpec((block, width), lambda i: (i, 0)),
            pl.BlockSpec((2, width), lambda i: (0, 0)),
        ],
        out_specs=pl.BlockSpec((block, width), lambda i: (i, 0)),
        out_shape=jax.ShapeDtypeStruct((rows, width), bf16),
        compiler_params=params(),
        cost_estimate=pl.CostEstimate(
            flops=10 * rows * width, bytes_accessed=4 * rows * width, transcendentals=rows
        ),
        name="layer_norm",
    )(frames, modulation)


def head_norm(x, gain_row):
    squares = jnp.mean(x * x, axis=-1, keepdims=True)
    return (x * lax.rsqrt(squares + 1e-06) * gain_row).astype(bf16)


def project_kernel(count, starts, kinds, columns, resumed, gain_ref, *refs):
    lefts, rights = refs[:count], refs[count : 2 * count]
    total_ref, refs = refs[2 * count] if resumed else None, refs[2 * count + resumed :]
    out_ref = refs[0]
    first, number = columns
    total = total_ref[:, first : first + number] if resumed else None
    for i in range(count):
        depth = rights[i].shape[0]
        left = lefts[i][...] if starts is None else lefts[i][:, pl.ds(starts()[i], depth)]
        part = dot(left, rights[i][:, first : first + number])
        total = part if total is None else total + part
    if kinds is None:
        out_ref[...] = total
        return
    for block, kind in enumerate(kinds):
        for head in range(HEADS):
            begin = block * WIDTH + head * HEAD_DIM
            x = total[:, begin : begin + HEAD_DIM]
            out_ref[:, begin : begin + HEAD_DIM] = (
                x.astype(bf16) if kind is None else head_norm(x, gain_ref[kind : kind + 1])
            )


def project(pairs, qk_gain, columns, name, starts=None, kinds=None, total=None):
    lefts, rights = [list(side) for side in zip(*pairs)]
    rows = lefts[0].shape[0]
    depth = sum(right.shape[0] for right in rights)
    resumed = total is not None
    operands = [qk_gain, *lefts, *rights] + [total] * resumed
    return pl.pallas_call(
        functools.partial(project_kernel, len(pairs), starts, kinds, columns, resumed),
        in_specs=[VMEM] * len(operands),
        out_specs=VMEM,
        out_shape=jax.ShapeDtypeStruct((rows, columns[1]), f32 if kinds is None else bf16),
        compiler_params=params(),
        cost_estimate=pl.CostEstimate(
            flops=2 * rows * depth * columns[1],
            bytes_accessed=2 * depth * (rows + columns[1]),
            transcendentals=rows,
        ),
        name=name,
    )(*operands)


def arrange_kernel(starts, order, homes, normed_ref, *out_refs):
    rows = normed_ref.shape[0]
    places, cores = starts()
    depth = normed_ref.shape[1] // lax.axis_size("fsdp")
    quarter = depth // 4
    source = lax.broadcasted_iota(jnp.int32, (depth, depth), 0)
    target = lax.broadcasted_iota(jnp.int32, (depth, depth), 1)
    for here in range(2):
        wanted = target
        for i, number in enumerate(order(cores[here])):
            inside = (target >= i * quarter) & (target < (i + 1) * quarter)
            wanted = jnp.where(inside, target + (number - i) * quarter, wanted)
        chosen = (source == wanted).astype(f32).astype(bf16)
        for slot, place in enumerate(places[here]):
            strip = normed_ref[:, pl.ds(pl.multiple_of(place, TILE), depth)]
            moved = dot(strip, chosen).astype(bf16)
            for i, (out, at) in enumerate(homes[slot]):
                out_refs[2 * out + here][:, at * quarter : (at + 1) * quarter] = moved[
                    :, i * quarter : (i + 1) * quarter
                ]


def arrange(starts, order, homes, widths, normed):
    rows = normed.shape[0]
    shapes = [jax.ShapeDtypeStruct((rows, width), bf16) for width in widths for _ in range(2)]
    return pl.pallas_call(
        functools.partial(arrange_kernel, starts, order, homes),
        in_specs=[VMEM],
        out_specs=[VMEM] * len(shapes),
        out_shape=shapes,
        compiler_params=params(),
        cost_estimate=pl.CostEstimate(
            flops=8 * rows * normed.shape[1] * TILE, bytes_accessed=4 * rows * normed.shape[1],
            transcendentals=0,
        ),
        name="arrange",
    )(normed)


def heads():
    for head in range(HEADS):
        ks = slice(head * HEAD_DIM, (head + 1) * HEAD_DIM)
        yield ks, slice(WIDTH + head * HEAD_DIM, WIDTH + (head + 1) * HEAD_DIM)


def share(query, keys, values, flag=None):
    raised = jnp.exp(dot_t(query, keys) * (1.0 / math.sqrt(HEAD_DIM)))
    if flag is not None:
        raised = raised * flag
    return dot(raised.astype(bf16), values), jnp.sum(raised, axis=-1, keepdims=True)


def attend_own_kernel(queries_ref, stacked_ref, weighted_ref, mass_ref):
    tiles = queries_ref.shape[0] // TILE
    for ks, vs in heads():
        for tile in range(tiles):
            rows = slice(tile * TILE, (tile + 1) * TILE)
            span = slice(max(tile - REACH, 0) * TILE, min(tile + REACH + 1, tiles) * TILE)
            weighted, mass = share(queries_ref[rows, ks], stacked_ref[span, ks], stacked_ref[span, vs])
            weighted_ref[rows, ks] = weighted
            mass_ref[rows, ks] = jnp.broadcast_to(mass, (TILE, HEAD_DIM))


def attend_own(queries, stacked):
    rows = queries.shape[0]
    return pl.pallas_call(
        attend_own_kernel,
        in_specs=[VMEM] * 2,
        out_specs=[VMEM] * 2,
        out_shape=[jax.ShapeDtypeStruct((rows, WIDTH), f32)] * 2,
        compiler_params=params(),
        cost_estimate=pl.CostEstimate(
            flops=4 * rows * rows * WIDTH, bytes_accessed=14 * rows * WIDTH,
            transcendentals=rows * rows * HEADS,
        ),
        name="attend_own_slab",
    )(queries, stacked)


def attend_kernel(layout, count, arrivals, queries_ref, weighted_ref, mass_ref, *refs):
    near_ref, arrived, refs = refs[0], refs[1:arrivals], refs[arrivals:]
    sources = refs[:count]
    mixed_ref, before, behind, attended, blocks, sems = refs[count:]
    tiles = queries_ref.shape[0] // TILE
    place = lax.axis_index("frame")
    far = arrived[0][...]
    for ref in arrived[1:]:
        far = far + ref[...]
    odd = (place & 1) == 1
    before[...] = jnp.where(odd, near_ref[...], far)
    behind[...] = jnp.where(odd, far, near_ref[...])
    has_before = (place > 0).astype(f32)
    has_behind = (place < lax.axis_size("frame") - 1).astype(f32)
    for ks, vs in heads():
        for tile in range(tiles):
            rows = slice(tile * TILE, (tile + 1) * TILE)
            weighted, mass = weighted_ref[rows, ks], mass_ref[rows, ks]
            low, high = tile - REACH, tile + REACH + 1 - tiles
            spans = []
            if low < 0:
                spans.append((before, slice((low + REACH) * TILE, BORDER), has_before))
            if high > 0:
                spans.append((behind, slice(0, high * TILE), has_behind))
            for ref, span, flag in spans:
                more, extra = share(queries_ref[rows, ks], ref[span, ks], ref[span, vs], flag)
                weighted, mass = weighted + more, mass + extra
            attended[rows, ks] = (weighted / mass).astype(bf16)
    width = blocks.shape[2]
    copies = []
    for number, (source, begin, place) in enumerate(layout()):
        blocks[number] = dot(attended[...], sources[source][:, begin : begin + width]).astype(bf16)
        copy = pltpu.make_async_copy(
            blocks.at[number],
            mixed_ref.at[0, :, pl.ds(pl.multiple_of(place, TILE), width)],
            sems.at[number],
        )
        copy.start()
        copies.append(copy)
    for copy in copies:
        copy.wait()


def attend(layout, sources, queries, own, edges, model):
    rows, number = queries.shape[0], len(layout())
    width = model // number
    return pl.pallas_call(
        functools.partial(attend_kernel, layout, len(sources), len(edges)),
        in_specs=[VMEM] * (3 + len(edges) + len(sources)),
        out_specs=ANY,
        out_shape=jax.ShapeDtypeStruct((1, rows, model), bf16),
        scratch_shapes=[
            pltpu.VMEM((BORDER, 2 * WIDTH), bf16),
            pltpu.VMEM((BORDER, 2 * WIDTH), bf16),
            pltpu.VMEM((rows, WIDTH), bf16),
            pltpu.VMEM((number, rows, width), bf16),
            pltpu.SemaphoreType.DMA((number,)),
        ],
        compiler_params=params(),
        cost_estimate=pl.CostEstimate(
            flops=2 * rows * WIDTH * (model + 4 * TILE),
            bytes_accessed=2 * (rows * model + WIDTH * model),
            transcendentals=rows * HEADS * 2 * TILE,
        ),
        name="attend_and_mix",
    )(queries, *own, *edges, *sources)


def swap(x, axis, bits):
    return lax.ppermute(x, axis, [(i, i ^ bits) for i in range(lax.axis_size(axis))])


def swap_plane(x, turn):
    places = lax.axis_size("frame")
    pairs = []
    for i in range(lax.axis_size("fsdp")):
        for j in range(places):
            pairs.append((i * places + j, i * places + (j ^ (1 + (i + turn) % 2))))
    return lax.ppermute(x, ("fsdp", "frame"), pairs)


def hop_order(chips):
    odd = [k for k in range(chips - 1, 0, -1) if k % 2]
    return odd + [k - 1 for k in odd if k > 1]


def halos(stacked):
    places = lax.axis_size("frame")
    odd = lax.axis_index("frame") & 1
    tail = stacked.shape[0] - BORDER
    near = lax.dynamic_slice_in_dim(stacked, (1 - odd) * tail, BORDER, 0)
    far = lax.dynamic_slice_in_dim(stacked, odd * tail, BORDER, 0)
    straight, out, on = [], [], []
    for i in range(lax.axis_size("fsdp")):
        for j in range(0, places, 4):
            for source, way, target in ((1, 3, 2), (2, 0, 1)):
                place = i * places + j
                if i % 2:
                    out.append((place + source, place + way))
                    on.append((place + way, place + target))
                else:
                    straight.append((place + source, place + target))
    axes = ("fsdp", "frame")
    way = lax.ppermute(far, axes, out)
    arrived = [lax.ppermute(way, axes, on), lax.ppermute(far, axes, straight)]
    if places > 4:
        pairs = [(j, j + 1) for j in range(3, places - 1, 4)]
        arrived.append(lax.ppermute(far, "frame", pairs + [(b, a) for a, b in pairs]))
    return [swap(near, "frame", 1)] + arrived


def split_plan(frames, modulation, w_qkv, w_out, qk_gain):
    chips = lax.axis_size("fsdp") // 2
    shard_rows, columns = w_qkv.shape
    shard_columns = w_out.shape[1]
    quarter = shard_rows // 4
    hops = hop_order(chips)
    odd, even = [k for k in hops if k % 2], [k for k in hops if k % 2 == 0]
    front, back = [k for k in odd if k > 1], even
    ring = [1] + front + back
    fence = lax.optimization_barrier

    def where():
        place, index = lax.axis_index("frame"), lax.axis_index("fsdp")
        high = (place >> 1) & 1
        return index // 2, index % 2, 2 * ((place & 1) ^ high) + high

    def order(core):
        spot = where()[2]
        return spot, spot ^ (2 + core), spot ^ (3 - core), spot ^ 1

    def shard_places():
        chip, core, _ = where()
        cores = (core, 1 - core)
        return [[((chip ^ k) * 2 + c) * shard_rows for k in ring] for c in cores], cores

    def own_places():
        chip, core, _ = where()
        return [pl.multiple_of((2 * chip + c) * shard_rows, TILE) for c in (core, 1 - core)]

    def out_layout():
        chip, core, _ = where()
        place = 2 * chip + core
        return [
            (source, 0, (place ^ (2 * k + here)) * shard_columns)
            for source, (k, here) in enumerate((k, here) for k in [0] + ring for here in (0, 1))
        ]

    spot = where()[2]
    part = lax.dynamic_slice_in_dim(w_qkv, spot * quarter, quarter, 0)
    come = [swap(part, "fsdp", 2 * k) for k in front]
    near = swap(part, "fsdp", 2)
    other_qkv = swap(w_qkv, "fsdp", 1)
    other_out = swap(w_out, "fsdp", 1)
    normed = norm_rows(frames, modulation)
    normed, come = fence((normed, come))

    late = [swap(x, "fsdp", 2) for x in come]
    one = jnp.concatenate(come, axis=0)
    one_rest = swap_plane(one, 0)
    nf, nb = len(front), len(back)
    homes = [[(4, nb), (5, 2 * nb), (2, 2 * nf + nb), (3, 0)]]
    homes += [[(0, i), (1, i), (2, i), (2, nf + i)] for i in range(nf)]
    homes += [[(4, i), (5, i), (2, 2 * nf + i), (5, nb + i)] for i in range(nb)]
    widths = [quarter * n for n in (nf, nf, 2 * nf + nb + 1, 1, nb + 1, 2 * nb + 1)]
    arranged = arrange(shard_places, order, homes, widths, normed)
    next_part = lax.dynamic_slice_in_dim(w_qkv, (spot ^ 1) * quarter, quarter, 0)
    one, one_rest, late, near, arranged, next_part = fence(
        (one, one_rest, late, near, arranged, next_part)
    )

    late = jnp.concatenate(late + [near], axis=0)
    two = swap_plane(jnp.concatenate([one, one_rest, late], axis=0), 1)
    across = swap(next_part, "fsdp", 2)
    cut = 2 * (shard_columns // TILE) // 3 * TILE
    wides = [swap(w_out[:, :cut], "fsdp", 2 * k) for k in front]
    total = project(
        [(normed, w_qkv), (normed, other_qkv)], qk_gain, (0, columns), "project_own", own_places
    )
    two, across, late, one, one_rest, wides, total = fence(
        (two, across, late, one, one_rest, wides, total)
    )

    relayed = two[2 * nf * quarter : (2 * nf + nb) * quarter]
    three = swap_plane(
        jnp.concatenate([late[: nb * quarter], relayed, late[nb * quarter :]], axis=0), 0
    )
    narrows = [swap(w_out[:, cut:], "fsdp", 2 * k) for k in front]
    pieces = []
    for x in (one, one_rest, two, across, late):
        pieces += [x, swap(x, "fsdp", 1)]
    total = project(
        list(zip(arranged[:10], pieces)), qk_gain, (0, columns), "project_mid", total=total
    )
    total, three, narrows = fence((total, three, narrows))

    last = [(arranged[10], three), (arranged[11], swap(three, "fsdp", 1))]
    stacked = project(
        last, qk_gain, (WIDTH, 2 * WIDTH), "project_keys_values", kinds=(1, None), total=total
    )
    queries = project(last, qk_gain, (0, WIDTH), "project_queries", kinds=(0,), total=total)

    joined = [jnp.concatenate(pair, axis=1) for pair in zip(wides, narrows)]
    sources = [w_out, other_out]
    edges = halos(stacked)
    for x in [swap(w_out, "fsdp", 2)] + joined + [swap(x, "fsdp", 2) for x in joined]:
        sources += [x, swap(fence((x, edges[0]))[0], "fsdp", 1)]
    return queries, stacked, edges, out_layout, sources


def whole_plan(frames, modulation, w_qkv, w_out, qk_gain):
    rows = lax.all_gather(w_qkv, "fsdp", axis=0, tiled=True)
    columns = lax.all_gather(w_out, "fsdp", axis=1, tiled=True)
    normed = norm_rows(frames, modulation)
    stacked = project(
        [(normed, rows)], qk_gain, (WIDTH, 2 * WIDTH), "project_keys_values", kinds=(1, None)
    )
    queries = project([(normed, rows)], qk_gain, (0, WIDTH), "project_queries", kinds=(0,))
    return queries, stacked, halos(stacked), lambda: [(0, i, i) for i in range(0, columns.shape[1], 3 * TILE)], [columns]


def on_device(frames, modulation, w_qkv, qk_gain, w_out):
    devices, places = lax.axis_size("fsdp"), lax.axis_size("frame")
    chips = devices // 2
    split = (
        devices % 2 == 0
        and chips > 2
        and chips & (chips - 1) == 0
        and w_qkv.shape[0] % TILE == 0
        and w_out.shape[1] % TILE == 0
    )
    plan = split_plan if split else whole_plan
    queries, stacked, edges, layout, sources = plan(
        frames[0], modulation[0], w_qkv, w_out, qk_gain
    )
    own = attend_own(queries, stacked)
    return attend(layout, sources, queries, own, edges, frames.shape[2])


def solution(mesh):
    return jax.shard_map(
        on_device,
        mesh=mesh,
        in_specs=(
            P("fsdp", "frame", None),
            P("fsdp", None, None),
            P("fsdp", None),
            P(),
            P(None, "fsdp"),
        ),
        out_specs=P("fsdp", "frame", None),
        check_vma=False,
    )
```

```python
import functools
import math

import jax
import jax.numpy as jnp
from jax import lax
from jax.experimental import pallas as pl
from jax.experimental.pallas import tpu as pltpu
from jax.sharding import PartitionSpec as P

HEAD_DIM = 128
HEADS = 2
WIDTH = HEADS * HEAD_DIM
TILE = 128
REACH = 2
BORDER = REACH * TILE
VMEM_BYTES = 40 * 1024 * 1024

f32 = jnp.float32
bf16 = jnp.bfloat16
ANY = pl.BlockSpec(memory_space=pl.ANY)
VMEM = pl.BlockSpec(memory_space=pltpu.VMEM)


def params():
    return pltpu.CompilerParams(vmem_limit_bytes=VMEM_BYTES)


def dot(a, b):
    return jnp.dot(a, b, preferred_element_type=f32)


def dot_t(a, b):
    return lax.dot_general(a, b, (((1,), (1,)), ((), ())), preferred_element_type=f32)


def norm_kernel(frames_ref, modulation_ref, normed_ref):
    values = frames_ref[...].astype(f32)
    average = jnp.mean(values, axis=-1, keepdims=True)
    centered = values - average
    spread = jnp.mean(centered * centered, axis=-1, keepdims=True)
    normed = centered * lax.rsqrt(spread + 1e-06)
    normed_ref[...] = (normed * (1.0 + modulation_ref[0:1]) + modulation_ref[1:2]).astype(bf16)


def norm_rows(frames, modulation):
    rows, width = frames.shape
    block = TILE // 2
    return pl.pallas_call(
        norm_kernel,
        grid=(rows // block,),
        in_specs=[
            pl.BlockSpec((block, width), lambda i: (i, 0)),
            pl.BlockSpec((2, width), lambda i: (0, 0)),
        ],
        out_specs=pl.BlockSpec((block, width), lambda i: (i, 0)),
        out_shape=jax.ShapeDtypeStruct((rows, width), bf16),
        compiler_params=params(),
        cost_estimate=pl.CostEstimate(
            flops=10 * rows * width, bytes_accessed=4 * rows * width, transcendentals=rows
        ),
        name="layer_norm",
    )(frames, modulation)


def head_norm(x, gain_row):
    squares = jnp.mean(x * x, axis=-1, keepdims=True)
    return (x * lax.rsqrt(squares + 1e-06) * gain_row).astype(bf16)


def project_kernel(count, starts, kinds, columns, resumed, gain_ref, *refs):
    lefts, rights = refs[:count], refs[count : 2 * count]
    total_ref, refs = refs[2 * count] if resumed else None, refs[2 * count + resumed :]
    out_ref = refs[0]
    first, number = columns
    total = total_ref[:, first : first + number] if resumed else None
    for i in range(count):
        depth = rights[i].shape[0]
        left = lefts[i][...] if starts is None else lefts[i][:, pl.ds(starts()[i], depth)]
        part = dot(left, rights[i][:, first : first + number])
        total = part if total is None else total + part
    if kinds is None:
        out_ref[...] = total
        return
    for block, kind in enumerate(kinds):
        for head in range(HEADS):
            begin = block * WIDTH + head * HEAD_DIM
            x = total[:, begin : begin + HEAD_DIM]
            out_ref[:, begin : begin + HEAD_DIM] = (
                x.astype(bf16) if kind is None else head_norm(x, gain_ref[kind : kind + 1])
            )


def project(pairs, qk_gain, columns, name, starts=None, kinds=None, total=None):
    lefts, rights = [list(side) for side in zip(*pairs)]
    rows = lefts[0].shape[0]
    depth = sum(right.shape[0] for right in rights)
    resumed = total is not None
    operands = [qk_gain, *lefts, *rights] + [total] * resumed
    return pl.pallas_call(
        functools.partial(project_kernel, len(pairs), starts, kinds, columns, resumed),
        in_specs=[VMEM] * len(operands),
        out_specs=VMEM,
        out_shape=jax.ShapeDtypeStruct((rows, columns[1]), f32 if kinds is None else bf16),
        compiler_params=params(),
        cost_estimate=pl.CostEstimate(
            flops=2 * rows * depth * columns[1],
            bytes_accessed=2 * depth * (rows + columns[1]),
            transcendentals=rows,
        ),
        name=name,
    )(*operands)


def arrange_kernel(starts, order, homes, normed_ref, *out_refs):
    rows = normed_ref.shape[0]
    places, cores = starts()
    depth = normed_ref.shape[1] // lax.axis_size("fsdp")
    quarter = depth // 4
    source = lax.broadcasted_iota(jnp.int32, (depth, depth), 0)
    target = lax.broadcasted_iota(jnp.int32, (depth, depth), 1)
    for here in range(2):
        wanted = target
        for i, number in enumerate(order(cores[here])):
            inside = (target >= i * quarter) & (target < (i + 1) * quarter)
            wanted = jnp.where(inside, target + (number - i) * quarter, wanted)
        chosen = (source == wanted).astype(f32).astype(bf16)
        for slot, place in enumerate(places[here]):
            strip = normed_ref[:, pl.ds(pl.multiple_of(place, TILE), depth)]
            moved = dot(strip, chosen).astype(bf16)
            for i, (out, at) in enumerate(homes[slot]):
                out_refs[2 * out + here][:, at * quarter : (at + 1) * quarter] = moved[
                    :, i * quarter : (i + 1) * quarter
                ]


def arrange(starts, order, homes, widths, normed):
    rows = normed.shape[0]
    shapes = [jax.ShapeDtypeStruct((rows, width), bf16) for width in widths for _ in range(2)]
    return pl.pallas_call(
        functools.partial(arrange_kernel, starts, order, homes),
        in_specs=[VMEM],
        out_specs=[VMEM] * len(shapes),
        out_shape=shapes,
        compiler_params=params(),
        cost_estimate=pl.CostEstimate(
            flops=8 * rows * normed.shape[1] * TILE, bytes_accessed=4 * rows * normed.shape[1],
            transcendentals=0,
        ),
        name="arrange",
    )(normed)


def heads():
    for head in range(HEADS):
        ks = slice(head * HEAD_DIM, (head + 1) * HEAD_DIM)
        yield ks, slice(WIDTH + head * HEAD_DIM, WIDTH + (head + 1) * HEAD_DIM)


def share(query, keys, values, flag=None):
    raised = jnp.exp(dot_t(query, keys) * (1.0 / math.sqrt(HEAD_DIM)))
    if flag is not None:
        raised = raised * flag
    return dot(raised.astype(bf16), values), jnp.sum(raised, axis=-1, keepdims=True)


def attend_own_kernel(queries_ref, stacked_ref, weighted_ref, mass_ref):
    tiles = queries_ref.shape[0] // TILE
    for ks, vs in heads():
        for tile in range(tiles):
            rows = slice(tile * TILE, (tile + 1) * TILE)
            span = slice(max(tile - REACH, 0) * TILE, min(tile + REACH + 1, tiles) * TILE)
            weighted, mass = share(queries_ref[rows, ks], stacked_ref[span, ks], stacked_ref[span, vs])
            weighted_ref[rows, ks] = weighted
            mass_ref[rows, ks] = jnp.broadcast_to(mass, (TILE, HEAD_DIM))


def attend_own(queries, stacked):
    rows = queries.shape[0]
    return pl.pallas_call(
        attend_own_kernel,
        in_specs=[VMEM] * 2,
        out_specs=[VMEM] * 2,
        out_shape=[jax.ShapeDtypeStruct((rows, WIDTH), f32)] * 2,
        compiler_params=params(),
        cost_estimate=pl.CostEstimate(
            flops=4 * rows * rows * WIDTH, bytes_accessed=14 * rows * WIDTH,
            transcendentals=rows * rows * HEADS,
        ),
        name="attend_own_slab",
    )(queries, stacked)


def attend_kernel(layout, count, arrivals, queries_ref, weighted_ref, mass_ref, *refs):
    near_ref, arrived, refs = refs[0], refs[1:arrivals], refs[arrivals:]
    sources = refs[:count]
    mixed_ref, before, behind, attended, blocks, sems = refs[count:]
    tiles = queries_ref.shape[0] // TILE
    place = lax.axis_index("frame")
    far = arrived[0][...]
    for ref in arrived[1:]:
        far = far + ref[...]
    odd = (place & 1) == 1
    before[...] = jnp.where(odd, near_ref[...], far)
    behind[...] = jnp.where(odd, far, near_ref[...])
    has_before = (place > 0).astype(f32)
    has_behind = (place < lax.axis_size("frame") - 1).astype(f32)
    for ks, vs in heads():
        for tile in range(tiles):
            rows = slice(tile * TILE, (tile + 1) * TILE)
            weighted, mass = weighted_ref[rows, ks], mass_ref[rows, ks]
            low, high = tile - REACH, tile + REACH + 1 - tiles
            spans = []
            if low < 0:
                spans.append((before, slice((low + REACH) * TILE, BORDER), has_before))
            if high > 0:
                spans.append((behind, slice(0, high * TILE), has_behind))
            for ref, span, flag in spans:
                more, extra = share(queries_ref[rows, ks], ref[span, ks], ref[span, vs], flag)
                weighted, mass = weighted + more, mass + extra
            attended[rows, ks] = (weighted / mass).astype(bf16)
    width = blocks.shape[2]
    copies = []
    for number, (source, begin, place) in enumerate(layout()):
        blocks[number] = dot(attended[...], sources[source][:, begin : begin + width]).astype(bf16)
        copy = pltpu.make_async_copy(
            blocks.at[number],
            mixed_ref.at[0, :, pl.ds(pl.multiple_of(place, TILE), width)],
            sems.at[number],
        )
        copy.start()
        copies.append(copy)
    for copy in copies:
        copy.wait()


def attend(layout, sources, queries, own, edges, model):
    rows, number = queries.shape[0], len(layout())
    width = model // number
    return pl.pallas_call(
        functools.partial(attend_kernel, layout, len(sources), len(edges)),
        in_specs=[VMEM] * (3 + len(edges) + len(sources)),
        out_specs=ANY,
        out_shape=jax.ShapeDtypeStruct((1, rows, model), bf16),
        scratch_shapes=[
            pltpu.VMEM((BORDER, 2 * WIDTH), bf16),
            pltpu.VMEM((BORDER, 2 * WIDTH), bf16),
            pltpu.VMEM((rows, WIDTH), bf16),
            pltpu.VMEM((number, rows, width), bf16),
            pltpu.SemaphoreType.DMA((number,)),
        ],
        compiler_params=params(),
        cost_estimate=pl.CostEstimate(
            flops=2 * rows * WIDTH * (model + 4 * TILE),
            bytes_accessed=2 * (rows * model + WIDTH * model),
            transcendentals=rows * HEADS * 2 * TILE,
        ),
        name="attend_and_mix",
    )(queries, *own, *edges, *sources)


def swap(x, axis, bits):
    return lax.ppermute(x, axis, [(i, i ^ bits) for i in range(lax.axis_size(axis))])


def swap_plane(x, turn):
    places = lax.axis_size("frame")
    pairs = []
    for i in range(lax.axis_size("fsdp")):
        for j in range(places):
            pairs.append((i * places + j, i * places + (j ^ (1 + (i + turn) % 2))))
    return lax.ppermute(x, ("fsdp", "frame"), pairs)


def hop_order(chips):
    odd = [k for k in range(chips - 1, 0, -1) if k % 2]
    return odd + [k - 1 for k in odd if k > 1]


def halos(stacked):
    places = lax.axis_size("frame")
    odd = lax.axis_index("frame") & 1
    tail = stacked.shape[0] - BORDER
    near = lax.dynamic_slice_in_dim(stacked, (1 - odd) * tail, BORDER, 0)
    far = lax.dynamic_slice_in_dim(stacked, odd * tail, BORDER, 0)
    straight, out, on = [], [], []
    for i in range(lax.axis_size("fsdp")):
        for j in range(0, places, 4):
            for source, way, target in ((1, 3, 2), (2, 0, 1)):
                place = i * places + j
                if i % 2:
                    out.append((place + source, place + way))
                    on.append((place + way, place + target))
                else:
                    straight.append((place + source, place + target))
    axes = ("fsdp", "frame")
    way = lax.ppermute(far, axes, out)
    arrived = [lax.ppermute(way, axes, on), lax.ppermute(far, axes, straight)]
    if places > 4:
        pairs = [(j, j + 1) for j in range(3, places - 1, 4)]
        arrived.append(lax.ppermute(far, "frame", pairs + [(b, a) for a, b in pairs]))
    return [swap(near, "frame", 1)] + arrived, way


def split_plan(frames, modulation, w_qkv, w_out, qk_gain):
    chips = lax.axis_size("fsdp") // 2
    shard_rows, columns = w_qkv.shape
    shard_columns = w_out.shape[1]
    quarter = shard_rows // 4
    hops = hop_order(chips)
    odd, even = [k for k in hops if k % 2], [k for k in hops if k % 2 == 0]
    front, back = [k for k in odd if k > 1], even
    ring = [1] + front + back
    fence = lax.optimization_barrier

    def where():
        place, index = lax.axis_index("frame"), lax.axis_index("fsdp")
        high = (place >> 1) & 1
        return index // 2, index % 2, 2 * ((place & 1) ^ high) + high

    def order(core):
        spot = where()[2]
        return spot, spot ^ (2 + core), spot ^ (3 - core), spot ^ 1

    def shard_places():
        chip, core, _ = where()
        cores = (core, 1 - core)
        return [[((chip ^ k) * 2 + c) * shard_rows for k in ring] for c in cores], cores

    def own_places():
        chip, core, _ = where()
        return [pl.multiple_of((2 * chip + c) * shard_rows, TILE) for c in (core, 1 - core)]

    def out_layout():
        chip, core, _ = where()
        place = 2 * chip + core
        return [
            (source, 0, (place ^ (2 * k + here)) * shard_columns)
            for source, (k, here) in enumerate((k, here) for k in [0] + ring for here in (0, 1))
        ]

    spot = where()[2]
    part = lax.dynamic_slice_in_dim(w_qkv, spot * quarter, quarter, 0)
    come = [swap(part, "fsdp", 2 * k) for k in front]
    near = swap(part, "fsdp", 2)
    other_qkv = swap(w_qkv, "fsdp", 1)
    other_out = swap(w_out, "fsdp", 1)
    normed = norm_rows(frames, modulation)
    normed, come = fence((normed, come))

    late = [swap(x, "fsdp", 2) for x in come]
    one = jnp.concatenate(come, axis=0)
    one_rest = swap_plane(one, 0)
    nf, nb = len(front), len(back)
    homes = [[(0, 2 * nf + nb), (2, 2 * nb), (1, 2 * nf + nb), (0, 2 * nf + nb + 1)]]
    homes += [[(0, i), (0, nf + i), (1, i), (1, nf + i)] for i in range(nf)]
    homes += [[(0, 2 * nf + i), (2, i), (1, 2 * nf + i), (2, nb + i)] for i in range(nb)]
    widths = [quarter * n for n in (2 * nf + nb + 2, 2 * nf + nb + 1, 2 * nb + 1)]
    arranged = arrange(shard_places, order, homes, widths, normed)
    next_part = lax.dynamic_slice_in_dim(w_qkv, (spot ^ 1) * quarter, quarter, 0)
    one, one_rest, late, near, arranged, next_part = fence(
        (one, one_rest, late, near, arranged, next_part)
    )

    late = jnp.concatenate(late + [near], axis=0)
    two = swap_plane(jnp.concatenate([one, one_rest, late], axis=0), 1)
    across = swap(next_part, "fsdp", 2)
    cut = 2 * (shard_columns // TILE) // 3 * TILE
    wides = [swap(w_out[:, :cut], "fsdp", 2 * k) for k in front]
    total = project(
        [(normed, w_qkv), (normed, other_qkv)], qk_gain, (0, columns), "project_own", own_places
    )
    two, across, late, one, one_rest, wides, total = fence(
        (two, across, late, one, one_rest, wides, total)
    )

    relayed = two[2 * nf * quarter : (2 * nf + nb) * quarter]
    three = swap_plane(
        jnp.concatenate([late[: nb * quarter], relayed, late[nb * quarter :]], axis=0), 0
    )
    narrows = [swap(w_out[:, cut:], "fsdp", 2 * k) for k in front]
    kept = jnp.concatenate([one, one_rest, late, across], axis=0)
    pieces = [kept, swap(kept, "fsdp", 1), two, swap(two, "fsdp", 1)]
    total = project(
        list(zip(arranged[:4], pieces)), qk_gain, (0, columns), "project_mid", total=total
    )
    total, three, narrows = fence((total, three, narrows))

    last = [(arranged[4], three), (arranged[5], swap(three, "fsdp", 1))]
    stacked = project(
        last, qk_gain, (WIDTH, 2 * WIDTH), "project_keys_values", kinds=(1, None), total=total
    )
    queries = project(last, qk_gain, (0, WIDTH), "project_queries", kinds=(0,), total=total)

    joined = [jnp.concatenate(pair, axis=1) for pair in zip(wides, narrows)]
    sources = [w_out, other_out]
    edges, way = halos(stacked)
    for x in [swap(w_out, "fsdp", 2)] + joined + [swap(x, "fsdp", 2) for x in joined]:
        sources += [x, swap(fence((x, way))[0], "fsdp", 1)]
    return queries, stacked, edges, out_layout, sources


def whole_plan(frames, modulation, w_qkv, w_out, qk_gain):
    rows = lax.all_gather(w_qkv, "fsdp", axis=0, tiled=True)
    columns = lax.all_gather(w_out, "fsdp", axis=1, tiled=True)
    normed = norm_rows(frames, modulation)
    stacked = project(
        [(normed, rows)], qk_gain, (WIDTH, 2 * WIDTH), "project_keys_values", kinds=(1, None)
    )
    queries = project([(normed, rows)], qk_gain, (0, WIDTH), "project_queries", kinds=(0,))
    return queries, stacked, halos(stacked)[0], lambda: [(0, i, i) for i in range(0, columns.shape[1], 3 * TILE)], [columns]


def on_device(frames, modulation, w_qkv, qk_gain, w_out):
    devices, places = lax.axis_size("fsdp"), lax.axis_size("frame")
    chips = devices // 2
    split = (
        devices % 2 == 0
        and chips > 2
        and chips & (chips - 1) == 0
        and w_qkv.shape[0] % TILE == 0
        and w_out.shape[1] % TILE == 0
    )
    plan = split_plan if split else whole_plan
    queries, stacked, edges, layout, sources = plan(
        frames[0], modulation[0], w_qkv, w_out, qk_gain
    )
    own = attend_own(queries, stacked)
    return attend(layout, sources, queries, own, edges, frames.shape[2])


def solution(mesh):
    return jax.shard_map(
        on_device,
        mesh=mesh,
        in_specs=(
            P("fsdp", "frame", None),
            P("fsdp", None, None),
            P("fsdp", None),
            P(),
            P(None, "fsdp"),
        ),
        out_specs=P("fsdp", "frame", None),
        check_vma=False,
    )
```

```python
import functools
import math

import jax
import jax.numpy as jnp
from jax import lax
from jax.experimental import pallas as pl
from jax.experimental.pallas import tpu as pltpu
from jax.sharding import PartitionSpec as P

HEAD_DIM = 128
HEADS = 2
WIDTH = HEADS * HEAD_DIM
TILE = 128
REACH = 2
BORDER = REACH * TILE
VMEM_BYTES = 40 * 1024 * 1024

f32 = jnp.float32
bf16 = jnp.bfloat16
ANY = pl.BlockSpec(memory_space=pl.ANY)
VMEM = pl.BlockSpec(memory_space=pltpu.VMEM)


def params():
    return pltpu.CompilerParams(vmem_limit_bytes=VMEM_BYTES)


def dot(a, b):
    return jnp.dot(a, b, preferred_element_type=f32)


def dot_t(a, b):
    return lax.dot_general(a, b, (((1,), (1,)), ((), ())), preferred_element_type=f32)


def norm_kernel(frames_ref, modulation_ref, normed_ref):
    values = frames_ref[...].astype(f32)
    average = jnp.mean(values, axis=-1, keepdims=True)
    centered = values - average
    spread = jnp.mean(centered * centered, axis=-1, keepdims=True)
    normed = centered * lax.rsqrt(spread + 1e-06)
    normed_ref[...] = (normed * (1.0 + modulation_ref[0:1]) + modulation_ref[1:2]).astype(bf16)


def norm_rows(frames, modulation):
    rows, width = frames.shape
    block = TILE // 2
    return pl.pallas_call(
        norm_kernel,
        grid=(rows // block,),
        in_specs=[
            pl.BlockSpec((block, width), lambda i: (i, 0)),
            pl.BlockSpec((2, width), lambda i: (0, 0)),
        ],
        out_specs=pl.BlockSpec((block, width), lambda i: (i, 0)),
        out_shape=jax.ShapeDtypeStruct((rows, width), bf16),
        compiler_params=params(),
        cost_estimate=pl.CostEstimate(
            flops=10 * rows * width, bytes_accessed=4 * rows * width, transcendentals=rows
        ),
        name="layer_norm",
    )(frames, modulation)


def head_norm(x, gain_row):
    squares = jnp.mean(x * x, axis=-1, keepdims=True)
    return (x * lax.rsqrt(squares + 1e-06) * gain_row).astype(bf16)


def project_kernel(count, starts, kinds, columns, resumed, gain_ref, *refs):
    lefts, rights = refs[:count], refs[count : 2 * count]
    total_ref, refs = refs[2 * count] if resumed else None, refs[2 * count + resumed :]
    out_ref = refs[0]
    first, number = columns
    total = total_ref[:, first : first + number] if resumed else None
    for i in range(count):
        depth = rights[i].shape[0]
        left = lefts[i][...] if starts is None else lefts[i][:, pl.ds(starts()[i], depth)]
        part = dot(left, rights[i][:, first : first + number])
        total = part if total is None else total + part
    if kinds is None:
        out_ref[...] = total
        return
    for block, kind in enumerate(kinds):
        for head in range(HEADS):
            begin = block * WIDTH + head * HEAD_DIM
            x = total[:, begin : begin + HEAD_DIM]
            out_ref[:, begin : begin + HEAD_DIM] = (
                x.astype(bf16) if kind is None else head_norm(x, gain_ref[kind : kind + 1])
            )


def project(pairs, qk_gain, columns, name, starts=None, kinds=None, total=None):
    lefts, rights = [list(side) for side in zip(*pairs)]
    rows = lefts[0].shape[0]
    depth = sum(right.shape[0] for right in rights)
    resumed = total is not None
    operands = [qk_gain, *lefts, *rights] + [total] * resumed
    return pl.pallas_call(
        functools.partial(project_kernel, len(pairs), starts, kinds, columns, resumed),
        in_specs=[VMEM] * len(operands),
        out_specs=VMEM,
        out_shape=jax.ShapeDtypeStruct((rows, columns[1]), f32 if kinds is None else bf16),
        compiler_params=params(),
        cost_estimate=pl.CostEstimate(
            flops=2 * rows * depth * columns[1],
            bytes_accessed=2 * depth * (rows + columns[1]),
            transcendentals=rows,
        ),
        name=name,
    )(*operands)


def arrange_kernel(starts, order, homes, normed_ref, *out_refs):
    rows = normed_ref.shape[0]
    places, cores = starts()
    depth = normed_ref.shape[1] // lax.axis_size("fsdp")
    quarter = depth // 4
    source = lax.broadcasted_iota(jnp.int32, (depth, depth), 0)
    target = lax.broadcasted_iota(jnp.int32, (depth, depth), 1)
    for here in range(2):
        wanted = target
        for i, number in enumerate(order(cores[here])):
            inside = (target >= i * quarter) & (target < (i + 1) * quarter)
            wanted = jnp.where(inside, target + (number - i) * quarter, wanted)
        chosen = (source == wanted).astype(f32).astype(bf16)
        for slot, place in enumerate(places[here]):
            strip = normed_ref[:, pl.ds(pl.multiple_of(place, TILE), depth)]
            moved = dot(strip, chosen).astype(bf16)
            for i, (out, at) in enumerate(homes[slot]):
                out_refs[2 * out + here][:, at * quarter : (at + 1) * quarter] = moved[
                    :, i * quarter : (i + 1) * quarter
                ]


def arrange(starts, order, homes, widths, normed):
    rows = normed.shape[0]
    shapes = [jax.ShapeDtypeStruct((rows, width), bf16) for width in widths for _ in range(2)]
    return pl.pallas_call(
        functools.partial(arrange_kernel, starts, order, homes),
        in_specs=[VMEM],
        out_specs=[VMEM] * len(shapes),
        out_shape=shapes,
        compiler_params=params(),
        cost_estimate=pl.CostEstimate(
            flops=8 * rows * normed.shape[1] * TILE, bytes_accessed=4 * rows * normed.shape[1],
            transcendentals=0,
        ),
        name="arrange",
    )(normed)


def heads():
    for head in range(HEADS):
        ks = slice(head * HEAD_DIM, (head + 1) * HEAD_DIM)
        yield ks, slice(WIDTH + head * HEAD_DIM, WIDTH + (head + 1) * HEAD_DIM)


def share(query, keys, values, flag=None):
    raised = jnp.exp(dot_t(query, keys) * (1.0 / math.sqrt(HEAD_DIM)))
    if flag is not None:
        raised = raised * flag
    return dot(raised.astype(bf16), values), jnp.sum(raised, axis=-1, keepdims=True)


def edge_span(tile, tiles, ahead):
    if ahead:
        return slice(0, max(tile + REACH + 1 - tiles, 0) * TILE)
    return slice(BORDER - max(REACH - tile, 0) * TILE, BORDER)


def edge_share(queries_ref, edge_ref, tile, tiles, ahead, ks, vs, flag=None):
    span = edge_span(tile, tiles, ahead)
    if span.start == span.stop:
        return None
    query = queries_ref[tile * TILE : (tile + 1) * TILE, ks]
    return share(query, edge_ref[span, ks], edge_ref[span, vs], flag)


def attend_own_kernel(queries_ref, stacked_ref, near_ref, weighted_ref, mass_ref):
    tiles = queries_ref.shape[0] // TILE
    place = lax.axis_index("frame")
    inside = ((place ^ 1) < lax.axis_size("frame")).astype(f32)
    for odd in (0, 1):

        @pl.when((place & 1) == odd)
        def _():
            for ks, vs in heads():
                for tile in range(tiles):
                    rows = slice(tile * TILE, (tile + 1) * TILE)
                    span = slice(max(tile - REACH, 0) * TILE, min(tile + REACH + 1, tiles) * TILE)
                    keys, values = stacked_ref[span, ks], stacked_ref[span, vs]
                    weighted, mass = share(queries_ref[rows, ks], keys, values)
                    more = edge_share(queries_ref, near_ref, tile, tiles, odd == 0, ks, vs, inside)
                    if more is not None:
                        weighted, mass = weighted + more[0], mass + more[1]
                    weighted_ref[rows, ks] = weighted
                    mass_ref[rows, ks] = jnp.broadcast_to(mass, (TILE, HEAD_DIM))


def attend_own(queries, stacked, near):
    rows = queries.shape[0]
    return pl.pallas_call(
        attend_own_kernel,
        in_specs=[VMEM] * 3,
        out_specs=[VMEM] * 2,
        out_shape=[jax.ShapeDtypeStruct((rows, WIDTH), f32)] * 2,
        compiler_params=params(),
        cost_estimate=pl.CostEstimate(
            flops=4 * rows * rows * WIDTH, bytes_accessed=14 * rows * WIDTH,
            transcendentals=rows * rows * HEADS,
        ),
        name="attend_own_slab",
    )(queries, stacked, near)


def attend_kernel(layout, count, arrivals, queries_ref, weighted_ref, mass_ref, *refs):
    arrived, refs = refs[:arrivals], refs[arrivals:]
    sources = refs[:count]
    mixed_ref, far, attended, blocks, sems = refs[count:]
    tiles = queries_ref.shape[0] // TILE
    place = lax.axis_index("frame")
    parity = place & 1
    exists = jnp.where(parity == 1, place < lax.axis_size("frame") - 1, place > 0)

    @pl.when(jnp.logical_not(exists))
    def _():
        attended[...] = (weighted_ref[...] / mass_ref[...]).astype(bf16)

    for odd in (0, 1):

        @pl.when(jnp.logical_and(exists, parity == odd))
        def _():
            total = arrived[0][...]
            for ref in arrived[1:]:
                total = total + ref[...]
            far[...] = total
            for ks, vs in heads():
                for tile in range(tiles):
                    rows = slice(tile * TILE, (tile + 1) * TILE)
                    weighted, mass = weighted_ref[rows, ks], mass_ref[rows, ks]
                    more = edge_share(queries_ref, far, tile, tiles, odd == 1, ks, vs)
                    if more is not None:
                        weighted, mass = weighted + more[0], mass + more[1]
                    attended[rows, ks] = (weighted / mass).astype(bf16)

    width = blocks.shape[2]
    copies = []
    for number, (source, begin, place) in enumerate(layout()):
        blocks[number] = dot(attended[...], sources[source][:, begin : begin + width]).astype(bf16)
        copy = pltpu.make_async_copy(
            blocks.at[number],
            mixed_ref.at[0, :, pl.ds(pl.multiple_of(place, TILE), width)],
            sems.at[number],
        )
        copy.start()
        copies.append(copy)
    for copy in copies:
        copy.wait()


def attend(layout, sources, queries, own, arrived, model):
    rows, number = queries.shape[0], len(layout())
    width = model // number
    return pl.pallas_call(
        functools.partial(attend_kernel, layout, len(sources), len(arrived)),
        in_specs=[VMEM] * (3 + len(arrived) + len(sources)),
        out_specs=ANY,
        out_shape=jax.ShapeDtypeStruct((1, rows, model), bf16),
        scratch_shapes=[
            pltpu.VMEM((BORDER, 2 * WIDTH), bf16),
            pltpu.VMEM((rows, WIDTH), bf16),
            pltpu.VMEM((number, rows, width), bf16),
            pltpu.SemaphoreType.DMA((number,)),
        ],
        compiler_params=params(),
        cost_estimate=pl.CostEstimate(
            flops=2 * rows * WIDTH * (model + 4 * TILE),
            bytes_accessed=2 * (rows * model + WIDTH * model),
            transcendentals=rows * HEADS * 2 * TILE,
        ),
        name="attend_and_mix",
    )(queries, *own, *arrived, *sources)


def swap(x, axis, bits):
    return lax.ppermute(x, axis, [(i, i ^ bits) for i in range(lax.axis_size(axis))])


def swap_plane(x, turn):
    places = lax.axis_size("frame")
    pairs = []
    for i in range(lax.axis_size("fsdp")):
        for j in range(places):
            pairs.append((i * places + j, i * places + (j ^ (1 + (i + turn) % 2))))
    return lax.ppermute(x, ("fsdp", "frame"), pairs)


def hop_order(chips):
    odd = [k for k in range(chips - 1, 0, -1) if k % 2]
    return odd + [k - 1 for k in odd if k > 1]


def halos(stacked):
    places = lax.axis_size("frame")
    odd = lax.axis_index("frame") & 1
    tail = stacked.shape[0] - BORDER
    near = lax.dynamic_slice_in_dim(stacked, (1 - odd) * tail, BORDER, 0)
    far = lax.dynamic_slice_in_dim(stacked, odd * tail, BORDER, 0)
    straight, out, on = [], [], []
    for i in range(lax.axis_size("fsdp")):
        for j in range(0, places, 4):
            for source, way, target in ((1, 3, 2), (2, 0, 1)):
                place = i * places + j
                if i % 2:
                    out.append((place + source, place + way))
                    on.append((place + way, place + target))
                else:
                    straight.append((place + source, place + target))
    axes = ("fsdp", "frame")
    way = lax.ppermute(far, axes, out)
    arrived = [lax.ppermute(way, axes, on), lax.ppermute(far, axes, straight)]
    if places > 4:
        pairs = [(j, j + 1) for j in range(3, places - 1, 4)]
        arrived.append(lax.ppermute(far, "frame", pairs + [(b, a) for a, b in pairs]))
    return [swap(near, "frame", 1)] + arrived, way


def split_plan(frames, modulation, w_qkv, w_out, qk_gain):
    chips = lax.axis_size("fsdp") // 2
    shard_rows, columns = w_qkv.shape
    shard_columns = w_out.shape[1]
    quarter = shard_rows // 4
    hops = hop_order(chips)
    odd, even = [k for k in hops if k % 2], [k for k in hops if k % 2 == 0]
    front, back = [k for k in odd if k > 1], even
    ring = [1] + front + back
    fence = lax.optimization_barrier

    def where():
        place, index = lax.axis_index("frame"), lax.axis_index("fsdp")
        high = (place >> 1) & 1
        return index // 2, index % 2, 2 * ((place & 1) ^ high) + high

    def order(core):
        spot = where()[2]
        return spot, spot ^ (2 + core), spot ^ (3 - core), spot ^ 1

    def shard_places():
        chip, core, _ = where()
        cores = (core, 1 - core)
        return [[((chip ^ k) * 2 + c) * shard_rows for k in ring] for c in cores], cores

    def own_places():
        chip, core, _ = where()
        return [pl.multiple_of((2 * chip + c) * shard_rows, TILE) for c in (core, 1 - core)]

    def out_layout():
        chip, core, _ = where()
        place = 2 * chip + core
        return [
            (source, 0, (place ^ (2 * k + here)) * shard_columns)
            for source, (k, here) in enumerate((k, here) for k in [0] + ring for here in (0, 1))
        ]

    spot = where()[2]
    part = lax.dynamic_slice_in_dim(w_qkv, spot * quarter, quarter, 0)
    come = [swap(part, "fsdp", 2 * k) for k in front]
    near = swap(part, "fsdp", 2)
    other_qkv = swap(w_qkv, "fsdp", 1)
    normed = norm_rows(frames, modulation)
    normed, come = fence((normed, come))

    late = [swap(x, "fsdp", 2) for x in come]
    one = jnp.concatenate(come, axis=0)
    one_rest = swap_plane(one, 0)
    nf, nb = len(front), len(back)
    homes = [[(0, 2 * nf + nb), (0, 2 * nf + nb + 2), (1, 2 * nf + nb), (0, 2 * nf + nb + 1)]]
    homes += [[(0, i), (0, nf + i), (1, i), (1, nf + i)] for i in range(nf)]
    homes += [[(0, 2 * nf + i), (2, i), (1, 2 * nf + i), (2, nb + i)] for i in range(nb)]
    widths = [quarter * n for n in (2 * nf + nb + 3, 2 * nf + nb + 1, 2 * nb)]
    arranged = arrange(shard_places, order, homes, widths, normed)
    next_part = lax.dynamic_slice_in_dim(w_qkv, (spot ^ 1) * quarter, quarter, 0)
    one, one_rest, late, near, arranged, next_part = fence(
        (one, one_rest, late, near, arranged, next_part)
    )

    late = jnp.concatenate(late + [near], axis=0)
    two = swap_plane(jnp.concatenate([one, one_rest, late], axis=0), 1)
    near_rest = swap_plane(near, 0)
    across = swap(next_part, "fsdp", 2)
    cut = 2 * (shard_columns // TILE) // 3 * TILE
    wides = [swap(w_out[:, :cut], "fsdp", 2 * k) for k in front]
    total = project(
        [(normed, w_qkv), (normed, other_qkv)], qk_gain, (0, columns), "project_own", own_places
    )
    two, near_rest, across, late, one, one_rest, wides, total = fence(
        (two, near_rest, across, late, one, one_rest, wides, total)
    )

    relayed = two[2 * nf * quarter : (2 * nf + nb) * quarter]
    three = swap_plane(jnp.concatenate([late[: nb * quarter], relayed], axis=0), 0)
    narrows = [swap(w_out[:, cut:], "fsdp", 2 * k) for k in front]
    kept = jnp.concatenate([one, one_rest, late, across, near_rest], axis=0)
    pieces = [kept, swap(kept, "fsdp", 1), two, swap(two, "fsdp", 1)]
    total = project(
        list(zip(arranged[:4], pieces)), qk_gain, (0, columns), "project_mid", total=total
    )
    other_out = swap(w_out, "fsdp", 1)
    total, three, narrows, other_out = fence((total, three, narrows, other_out))

    last = [(arranged[4], three), (arranged[5], swap(three, "fsdp", 1))]
    stacked = project(
        last, qk_gain, (WIDTH, 2 * WIDTH), "project_keys_values", kinds=(1, None), total=total
    )
    queries = project(last, qk_gain, (0, WIDTH), "project_queries", kinds=(0,), total=total)

    joined = [jnp.concatenate(pair, axis=1) for pair in zip(wides, narrows)]
    sources = [w_out, other_out]
    edges, way = halos(stacked)
    for x in [swap(w_out, "fsdp", 2)] + joined + [swap(x, "fsdp", 2) for x in joined]:
        sources += [x, swap(fence((x, way))[0], "fsdp", 1)]
    return queries, stacked, edges, out_layout, sources


def whole_plan(frames, modulation, w_qkv, w_out, qk_gain):
    rows = lax.all_gather(w_qkv, "fsdp", axis=0, tiled=True)
    columns = lax.all_gather(w_out, "fsdp", axis=1, tiled=True)
    normed = norm_rows(frames, modulation)
    stacked = project(
        [(normed, rows)], qk_gain, (WIDTH, 2 * WIDTH), "project_keys_values", kinds=(1, None)
    )
    queries = project([(normed, rows)], qk_gain, (0, WIDTH), "project_queries", kinds=(0,))
    return queries, stacked, halos(stacked)[0], lambda: [(0, i, i) for i in range(0, columns.shape[1], 3 * TILE)], [columns]


def on_device(frames, modulation, w_qkv, qk_gain, w_out):
    devices, places = lax.axis_size("fsdp"), lax.axis_size("frame")
    chips = devices // 2
    split = (
        devices % 2 == 0
        and chips > 2
        and chips & (chips - 1) == 0
        and w_qkv.shape[0] % TILE == 0
        and w_out.shape[1] % TILE == 0
    )
    plan = split_plan if split else whole_plan
    queries, stacked, edges, layout, sources = plan(
        frames[0], modulation[0], w_qkv, w_out, qk_gain
    )
    own = attend_own(queries, stacked, edges[0])
    return attend(layout, sources, queries, own, edges[1:], frames.shape[2])


def solution(mesh):
    return jax.shard_map(
        on_device,
        mesh=mesh,
        in_specs=(
            P("fsdp", "frame", None),
            P("fsdp", None, None),
            P("fsdp", None),
            P(),
            P(None, "fsdp"),
        ),
        out_specs=P("fsdp", "frame", None),
        check_vma=False,
    )
```

```python
import functools
import math

import jax
import jax.numpy as jnp
from jax import lax
from jax.experimental import pallas as pl
from jax.experimental.pallas import tpu as pltpu
from jax.sharding import PartitionSpec as P

HEAD_DIM = 128
HEADS = 2
WIDTH = HEADS * HEAD_DIM
TILE = 128
REACH = 2
BORDER = REACH * TILE
VMEM_BYTES = 40 * 1024 * 1024

f32 = jnp.float32
bf16 = jnp.bfloat16
ANY = pl.BlockSpec(memory_space=pl.ANY)
VMEM = pl.BlockSpec(memory_space=pltpu.VMEM)


def params():
    return pltpu.CompilerParams(vmem_limit_bytes=VMEM_BYTES)


def dot(a, b):
    return jnp.dot(a, b, preferred_element_type=f32)


def dot_t(a, b):
    return lax.dot_general(a, b, (((1,), (1,)), ((), ())), preferred_element_type=f32)


def norm_kernel(frames_ref, modulation_ref, normed_ref):
    values = frames_ref[...].astype(f32)
    average = jnp.mean(values, axis=-1, keepdims=True)
    centered = values - average
    spread = jnp.mean(centered * centered, axis=-1, keepdims=True)
    normed = centered * lax.rsqrt(spread + 1e-06)
    normed_ref[...] = (normed * (1.0 + modulation_ref[0:1]) + modulation_ref[1:2]).astype(bf16)


def norm_rows(frames, modulation):
    rows, width = frames.shape
    block = TILE // 2
    return pl.pallas_call(
        norm_kernel,
        grid=(rows // block,),
        in_specs=[
            pl.BlockSpec((block, width), lambda i: (i, 0)),
            pl.BlockSpec((2, width), lambda i: (0, 0)),
        ],
        out_specs=pl.BlockSpec((block, width), lambda i: (i, 0)),
        out_shape=jax.ShapeDtypeStruct((rows, width), bf16),
        compiler_params=params(),
        cost_estimate=pl.CostEstimate(
            flops=10 * rows * width, bytes_accessed=4 * rows * width, transcendentals=rows
        ),
        name="layer_norm",
    )(frames, modulation)


def head_norm(x, gain_row):
    squares = jnp.mean(x * x, axis=-1, keepdims=True)
    return (x * lax.rsqrt(squares + 1e-06) * gain_row).astype(bf16)


def project_kernel(count, starts, kinds, columns, resumed, gain_ref, *refs):
    lefts, rights = refs[:count], refs[count : 2 * count]
    total_ref, refs = refs[2 * count] if resumed else None, refs[2 * count + resumed :]
    out_ref = refs[0]
    first, number = columns
    total = total_ref[:, first : first + number] if resumed else None
    for i in range(count):
        depth = rights[i].shape[0]
        left = lefts[i][...] if starts is None else lefts[i][:, pl.ds(starts()[i], depth)]
        part = dot(left, rights[i][:, first : first + number])
        total = part if total is None else total + part
    if kinds is None:
        out_ref[...] = total
        return
    for block, kind in enumerate(kinds):
        for head in range(HEADS):
            begin = block * WIDTH + head * HEAD_DIM
            x = total[:, begin : begin + HEAD_DIM]
            out_ref[:, begin : begin + HEAD_DIM] = (
                x.astype(bf16) if kind is None else head_norm(x, gain_ref[kind : kind + 1])
            )


def project(pairs, qk_gain, columns, name, starts=None, kinds=None, total=None):
    lefts, rights = [list(side) for side in zip(*pairs)]
    rows = lefts[0].shape[0]
    depth = sum(right.shape[0] for right in rights)
    resumed = total is not None
    operands = [qk_gain, *lefts, *rights] + [total] * resumed
    return pl.pallas_call(
        functools.partial(project_kernel, len(pairs), starts, kinds, columns, resumed),
        in_specs=[VMEM] * len(operands),
        out_specs=VMEM,
        out_shape=jax.ShapeDtypeStruct((rows, columns[1]), f32 if kinds is None else bf16),
        compiler_params=params(),
        cost_estimate=pl.CostEstimate(
            flops=2 * rows * depth * columns[1],
            bytes_accessed=2 * depth * (rows + columns[1]),
            transcendentals=rows,
        ),
        name=name,
    )(*operands)


def arrange_kernel(starts, order, homes, normed_ref, *out_refs):
    rows = normed_ref.shape[0]
    places, cores = starts()
    depth = normed_ref.shape[1] // lax.axis_size("fsdp")
    quarter = depth // 4
    source = lax.broadcasted_iota(jnp.int32, (depth, depth), 0)
    target = lax.broadcasted_iota(jnp.int32, (depth, depth), 1)
    for here in range(2):
        wanted = target
        for i, number in enumerate(order(cores[here])):
            inside = (target >= i * quarter) & (target < (i + 1) * quarter)
            wanted = jnp.where(inside, target + (number - i) * quarter, wanted)
        chosen = (source == wanted).astype(f32).astype(bf16)
        for slot, place in enumerate(places[here]):
            strip = normed_ref[:, pl.ds(pl.multiple_of(place, TILE), depth)]
            moved = dot(strip, chosen).astype(bf16)
            for i, (out, at) in enumerate(homes[slot]):
                out_refs[2 * out + here][:, at * quarter : (at + 1) * quarter] = moved[
                    :, i * quarter : (i + 1) * quarter
                ]


def arrange(starts, order, homes, widths, normed):
    rows = normed.shape[0]
    shapes = [jax.ShapeDtypeStruct((rows, width), bf16) for width in widths for _ in range(2)]
    return pl.pallas_call(
        functools.partial(arrange_kernel, starts, order, homes),
        in_specs=[VMEM],
        out_specs=[VMEM] * len(shapes),
        out_shape=shapes,
        compiler_params=params(),
        cost_estimate=pl.CostEstimate(
            flops=8 * rows * normed.shape[1] * TILE, bytes_accessed=4 * rows * normed.shape[1],
            transcendentals=0,
        ),
        name="arrange",
    )(normed)


def heads():
    for head in range(HEADS):
        ks = slice(head * HEAD_DIM, (head + 1) * HEAD_DIM)
        yield ks, slice(WIDTH + head * HEAD_DIM, WIDTH + (head + 1) * HEAD_DIM)


def share(query, keys, values, flag=None):
    raised = jnp.exp(dot_t(query, keys) * (1.0 / math.sqrt(HEAD_DIM)))
    if flag is not None:
        raised = raised * flag
    return dot(raised.astype(bf16), values), jnp.sum(raised, axis=-1, keepdims=True)


def edge_span(tile, tiles, ahead):
    if ahead:
        return slice(0, max(tile + REACH + 1 - tiles, 0) * TILE)
    return slice(BORDER - max(REACH - tile, 0) * TILE, BORDER)


def edge_share(queries_ref, edge_ref, tile, tiles, ahead, ks, vs, flag=None):
    span = edge_span(tile, tiles, ahead)
    if span.start == span.stop:
        return None
    query = queries_ref[tile * TILE : (tile + 1) * TILE, ks]
    return share(query, edge_ref[span, ks], edge_ref[span, vs], flag)


def attend_own_kernel(queries_ref, stacked_ref, near_ref, weighted_ref, mass_ref):
    tiles = queries_ref.shape[0] // TILE
    place = lax.axis_index("frame")
    inside = ((place ^ 1) < lax.axis_size("frame")).astype(f32)
    for odd in (0, 1):

        @pl.when((place & 1) == odd)
        def _():
            for ks, vs in heads():
                for tile in range(tiles):
                    rows = slice(tile * TILE, (tile + 1) * TILE)
                    span = slice(max(tile - REACH, 0) * TILE, min(tile + REACH + 1, tiles) * TILE)
                    keys, values = stacked_ref[span, ks], stacked_ref[span, vs]
                    weighted, mass = share(queries_ref[rows, ks], keys, values)
                    more = edge_share(queries_ref, near_ref, tile, tiles, odd == 0, ks, vs, inside)
                    if more is not None:
                        weighted, mass = weighted + more[0], mass + more[1]
                    weighted_ref[rows, ks] = weighted
                    mass_ref[rows, ks] = jnp.broadcast_to(mass, (TILE, HEAD_DIM))


def attend_own(queries, stacked, near):
    rows = queries.shape[0]
    return pl.pallas_call(
        attend_own_kernel,
        in_specs=[VMEM] * 3,
        out_specs=[VMEM] * 2,
        out_shape=[jax.ShapeDtypeStruct((rows, WIDTH), f32)] * 2,
        compiler_params=params(),
        cost_estimate=pl.CostEstimate(
            flops=4 * rows * rows * WIDTH, bytes_accessed=14 * rows * WIDTH,
            transcendentals=rows * rows * HEADS,
        ),
        name="attend_own_slab",
    )(queries, stacked, near)


def mix(layout, sources, attended, rows, blocks, sems, mixed_ref):
    width, copies = blocks.shape[2], []
    for number, (source, begin, place) in enumerate(layout()):
        held = sources[source][:, begin : begin + width]
        blocks[number, rows] = dot(attended[rows], held).astype(bf16)
        copy = pltpu.make_async_copy(
            blocks.at[number, rows],
            mixed_ref.at[0, rows, pl.ds(pl.multiple_of(place, TILE), width)],
            sems.at[number],
        )
        copy.start()
        copies.append(copy)
    return copies


def attend_kernel(layout, count, arrivals, queries_ref, weighted_ref, mass_ref, *refs):
    arrived, refs = refs[:arrivals], refs[arrivals:]
    sources = refs[:count]
    mixed_ref, far, attended, blocks, sems, late_sems = refs[count:]
    tiles = queries_ref.shape[0] // TILE
    place = lax.axis_index("frame")
    parity = place & 1
    exists = jnp.where(parity == 1, place < lax.axis_size("frame") - 1, place > 0)

    @pl.when(jnp.logical_not(exists))
    def _():
        attended[...] = (weighted_ref[...] / mass_ref[...]).astype(bf16)
        whole = slice(0, tiles * TILE)
        for copy in mix(layout, sources, attended, whole, blocks, sems, mixed_ref):
            copy.wait()

    for odd in (0, 1):
        spans = [edge_span(tile, tiles, odd == 1) for tile in range(tiles)]
        waiting = [tile for tile in range(tiles) if spans[tile].start != spans[tile].stop]
        ready = [tile for tile in range(tiles) if tile not in waiting]

        @pl.when(jnp.logical_and(exists, parity == odd))
        def _():
            copies = []
            if ready:
                rows = slice(ready[0] * TILE, (ready[-1] + 1) * TILE)
                attended[rows] = (weighted_ref[rows] / mass_ref[rows]).astype(bf16)
                copies += mix(layout, sources, attended, rows, blocks, sems, mixed_ref)
            total = arrived[0][...]
            for ref in arrived[1:]:
                total = total + ref[...]
            far[...] = total
            for ks, vs in heads():
                for tile in waiting:
                    rows = slice(tile * TILE, (tile + 1) * TILE)
                    more, extra = edge_share(queries_ref, far, tile, tiles, odd == 1, ks, vs)
                    weighted, mass = weighted_ref[rows, ks] + more, mass_ref[rows, ks] + extra
                    attended[rows, ks] = (weighted / mass).astype(bf16)
            rows = slice(waiting[0] * TILE, (waiting[-1] + 1) * TILE)
            copies += mix(layout, sources, attended, rows, blocks, late_sems, mixed_ref)
            for copy in copies:
                copy.wait()


def attend(layout, sources, queries, own, arrived, model):
    rows, number = queries.shape[0], len(layout())
    width = model // number
    return pl.pallas_call(
        functools.partial(attend_kernel, layout, len(sources), len(arrived)),
        in_specs=[VMEM] * (3 + len(arrived) + len(sources)),
        out_specs=ANY,
        out_shape=jax.ShapeDtypeStruct((1, rows, model), bf16),
        scratch_shapes=[
            pltpu.VMEM((BORDER, 2 * WIDTH), bf16),
            pltpu.VMEM((rows, WIDTH), bf16),
            pltpu.VMEM((number, rows, width), bf16),
            pltpu.SemaphoreType.DMA((number,)),
            pltpu.SemaphoreType.DMA((number,)),
        ],
        compiler_params=params(),
        cost_estimate=pl.CostEstimate(
            flops=2 * rows * WIDTH * (model + 4 * TILE),
            bytes_accessed=2 * (rows * model + WIDTH * model),
            transcendentals=rows * HEADS * 2 * TILE,
        ),
        name="attend_and_mix",
    )(queries, *own, *arrived, *sources)


def swap(x, axis, bits):
    return lax.ppermute(x, axis, [(i, i ^ bits) for i in range(lax.axis_size(axis))])


def swap_plane(x, turn):
    places = lax.axis_size("frame")
    pairs = []
    for i in range(lax.axis_size("fsdp")):
        for j in range(places):
            pairs.append((i * places + j, i * places + (j ^ (1 + (i + turn) % 2))))
    return lax.ppermute(x, ("fsdp", "frame"), pairs)


def hop_order(chips):
    odd = [k for k in range(chips - 1, 0, -1) if k % 2]
    return odd + [k - 1 for k in odd if k > 1]


def halos(stacked):
    places = lax.axis_size("frame")
    odd = lax.axis_index("frame") & 1
    tail = stacked.shape[0] - BORDER
    near = lax.dynamic_slice_in_dim(stacked, (1 - odd) * tail, BORDER, 0)
    far = lax.dynamic_slice_in_dim(stacked, odd * tail, BORDER, 0)
    axes = ("fsdp", "frame")
    straight, out, on = [], [], []
    for i in range(lax.axis_size("fsdp")):
        for j in range(0, places - 3, 4):
            for source, way, target in ((1, 3, 2), (2, 0, 1)):
                place = i * places + j
                if i % 2:
                    out.append((place + source, place + way))
                    on.append((place + way, place + target))
                else:
                    straight.append((place + source, place + target))
    way = lax.ppermute(far, axes, out)
    arrived = [lax.ppermute(way, axes, on), lax.ppermute(far, axes, straight)]
    rest = [j for j in range(1, places - 1, 2) if j % 4 == 3 or j >= places // 4 * 4]
    if rest:
        arrived.append(
            lax.ppermute(far, "frame", [(j, j + 1) for j in rest] + [(j + 1, j) for j in rest])
        )
    near_pairs = [(j, j ^ 1) for j in range(places) if j ^ 1 < places]
    return [lax.ppermute(near, "frame", near_pairs)] + arrived, way


def split_plan(frames, modulation, w_qkv, w_out, qk_gain):
    chips = lax.axis_size("fsdp") // 2
    shard_rows, columns = w_qkv.shape
    shard_columns = w_out.shape[1]
    quarter = shard_rows // 4
    hops = hop_order(chips)
    odd, even = [k for k in hops if k % 2], [k for k in hops if k % 2 == 0]
    front, back = [k for k in odd if k > 1], even
    ring = [1] + front + back
    fence = lax.optimization_barrier

    def where():
        place, index = lax.axis_index("frame"), lax.axis_index("fsdp")
        high = (place >> 1) & 1
        return index // 2, index % 2, 2 * ((place & 1) ^ high) + high

    def order(core):
        spot = where()[2]
        return spot, spot ^ (2 + core), spot ^ (3 - core), spot ^ 1

    def shard_places():
        chip, core, _ = where()
        cores = (core, 1 - core)
        return [[((chip ^ k) * 2 + c) * shard_rows for k in ring] for c in cores], cores

    def own_places():
        chip, core, _ = where()
        return [pl.multiple_of((2 * chip + c) * shard_rows, TILE) for c in (core, 1 - core)]

    def out_layout():
        chip, core, _ = where()
        place = 2 * chip + core
        return [
            (source, 0, (place ^ (2 * k + here)) * shard_columns)
            for source, (k, here) in enumerate((k, here) for k in [0] + ring for here in (0, 1))
        ]

    spot = where()[2]
    part = lax.dynamic_slice_in_dim(w_qkv, spot * quarter, quarter, 0)
    come = [swap(part, "fsdp", 2 * k) for k in front]
    near = swap(part, "fsdp", 2)
    other_qkv = swap(w_qkv, "fsdp", 1)
    normed = norm_rows(frames, modulation)
    normed, come = fence((normed, come))

    late = [swap(x, "fsdp", 2) for x in come]
    one = jnp.concatenate(come, axis=0)
    one_rest = swap_plane(one, 0)
    nf, nb = len(front), len(back)
    homes = [[(0, 2 * nf + nb), (0, 2 * nf + nb + 2), (1, 2 * nf + nb), (0, 2 * nf + nb + 1)]]
    homes += [[(0, i), (0, nf + i), (1, i), (1, nf + i)] for i in range(nf)]
    homes += [[(0, 2 * nf + i), (2, i), (1, 2 * nf + i), (2, nb + i)] for i in range(nb)]
    widths = [quarter * n for n in (2 * nf + nb + 3, 2 * nf + nb + 1, 2 * nb)]
    arranged = arrange(shard_places, order, homes, widths, normed)
    next_part = lax.dynamic_slice_in_dim(w_qkv, (spot ^ 1) * quarter, quarter, 0)
    one, one_rest, late, near, arranged, next_part = fence(
        (one, one_rest, late, near, arranged, next_part)
    )

    late = jnp.concatenate(late + [near], axis=0)
    two = swap_plane(jnp.concatenate([one, one_rest, late], axis=0), 1)
    near_rest = swap_plane(near, 0)
    across = swap(next_part, "fsdp", 2)
    cut = 2 * (shard_columns // TILE) // 3 * TILE
    wides = [swap(w_out[:, :cut], "fsdp", 2 * k) for k in front]
    total = project(
        [(normed, w_qkv), (normed, other_qkv)], qk_gain, (0, columns), "project_own", own_places
    )
    two, near_rest, across, late, one, one_rest, wides, total = fence(
        (two, near_rest, across, late, one, one_rest, wides, total)
    )

    relayed = two[2 * nf * quarter : (2 * nf + nb) * quarter]
    three = swap_plane(jnp.concatenate([late[: nb * quarter], relayed], axis=0), 0)
    narrows = [swap(w_out[:, cut:], "fsdp", 2 * k) for k in front]
    kept = jnp.concatenate([one, one_rest, late, across, near_rest], axis=0)
    pieces = [kept, swap(kept, "fsdp", 1), two, swap(two, "fsdp", 1)]
    total = project(
        list(zip(arranged[:4], pieces)), qk_gain, (0, columns), "project_mid", total=total
    )
    other_out = swap(w_out, "fsdp", 1)
    total, three, narrows, other_out = fence((total, three, narrows, other_out))

    last = [(arranged[4], three), (arranged[5], swap(three, "fsdp", 1))]
    stacked = project(
        last, qk_gain, (WIDTH, 2 * WIDTH), "project_keys_values", kinds=(1, None), total=total
    )
    queries = project(last, qk_gain, (0, WIDTH), "project_queries", kinds=(0,), total=total)

    joined = [jnp.concatenate(pair, axis=1) for pair in zip(wides, narrows)]
    sources = [w_out, other_out]
    edges, way = halos(stacked)
    for x in [swap(w_out, "fsdp", 2)] + joined + [swap(x, "fsdp", 2) for x in joined]:
        sources += [x, swap(fence((x, way))[0], "fsdp", 1)]
    return queries, stacked, edges, out_layout, sources


def whole_plan(frames, modulation, w_qkv, w_out, qk_gain):
    rows = lax.all_gather(w_qkv, "fsdp", axis=0, tiled=True)
    columns = lax.all_gather(w_out, "fsdp", axis=1, tiled=True)
    normed = norm_rows(frames, modulation)
    stacked = project(
        [(normed, rows)], qk_gain, (WIDTH, 2 * WIDTH), "project_keys_values", kinds=(1, None)
    )
    queries = project([(normed, rows)], qk_gain, (0, WIDTH), "project_queries", kinds=(0,))
    return queries, stacked, halos(stacked)[0], lambda: [(0, i, i) for i in range(0, columns.shape[1], 3 * TILE)], [columns]


def on_device(frames, modulation, w_qkv, qk_gain, w_out):
    devices, places = lax.axis_size("fsdp"), lax.axis_size("frame")
    chips = devices // 2
    split = (
        devices % 2 == 0
        and chips > 2
        and chips & (chips - 1) == 0
        and w_qkv.shape[0] % TILE == 0
        and w_out.shape[1] % TILE == 0
    )
    plan = split_plan if split else whole_plan
    queries, stacked, edges, layout, sources = plan(
        frames[0], modulation[0], w_qkv, w_out, qk_gain
    )
    own = attend_own(queries, stacked, edges[0])
    return attend(layout, sources, queries, own, edges[1:], frames.shape[2])


def solution(mesh):
    return jax.shard_map(
        on_device,
        mesh=mesh,
        in_specs=(
            P("fsdp", "frame", None),
            P("fsdp", None, None),
            P("fsdp", None),
            P(),
            P(None, "fsdp"),
        ),
        out_specs=P("fsdp", "frame", None),
        check_vma=False,
    )
```

```python
import functools
import math

import jax
import jax.numpy as jnp
from jax import lax
from jax.experimental import pallas as pl
from jax.experimental.pallas import tpu as pltpu
from jax.sharding import PartitionSpec as P

HEAD_DIM = 128
HEADS = 2
WIDTH = HEADS * HEAD_DIM
TILE = 128
REACH = 2
BORDER = REACH * TILE
VMEM_BYTES = 40 * 1024 * 1024

f32 = jnp.float32
bf16 = jnp.bfloat16
ANY = pl.BlockSpec(memory_space=pl.ANY)
VMEM = pl.BlockSpec(memory_space=pltpu.VMEM)


def params():
    return pltpu.CompilerParams(vmem_limit_bytes=VMEM_BYTES)


def dot(a, b):
    return jnp.dot(a, b, preferred_element_type=f32)


def dot_t(a, b):
    return lax.dot_general(a, b, (((1,), (1,)), ((), ())), preferred_element_type=f32)


def norm_kernel(frames_ref, modulation_ref, normed_ref):
    values = frames_ref[...].astype(f32)
    average = jnp.mean(values, axis=-1, keepdims=True)
    centered = values - average
    spread = jnp.mean(centered * centered, axis=-1, keepdims=True)
    normed = centered * lax.rsqrt(spread + 1e-06)
    normed_ref[...] = (normed * (1.0 + modulation_ref[0:1]) + modulation_ref[1:2]).astype(bf16)


def norm_rows(frames, modulation):
    rows, width = frames.shape
    block = TILE // 2
    return pl.pallas_call(
        norm_kernel,
        grid=(rows // block,),
        in_specs=[
            pl.BlockSpec((block, width), lambda i: (i, 0)),
            pl.BlockSpec((2, width), lambda i: (0, 0)),
        ],
        out_specs=pl.BlockSpec((block, width), lambda i: (i, 0)),
        out_shape=jax.ShapeDtypeStruct((rows, width), bf16),
        compiler_params=params(),
        cost_estimate=pl.CostEstimate(
            flops=10 * rows * width, bytes_accessed=4 * rows * width, transcendentals=rows
        ),
        name="layer_norm",
    )(frames, modulation)


def head_norm(x, gain_row):
    squares = jnp.mean(x * x, axis=-1, keepdims=True)
    return (x * lax.rsqrt(squares + 1e-06) * gain_row).astype(bf16)


def project_kernel(count, starts, kinds, columns, resumed, gain_ref, *refs):
    lefts, rights = refs[:count], refs[count : 2 * count]
    total_ref, refs = refs[2 * count] if resumed else None, refs[2 * count + resumed :]
    out_ref = refs[0]
    first, number = columns
    total = total_ref[:, first : first + number] if resumed else None
    for i in range(count):
        depth = rights[i].shape[0]
        left = lefts[i][...] if starts is None else lefts[i][:, pl.ds(starts()[i], depth)]
        part = dot(left, rights[i][:, first : first + number])
        total = part if total is None else total + part
    if kinds is None:
        out_ref[...] = total
        return
    for block, kind in enumerate(kinds):
        for head in range(HEADS):
            begin = block * WIDTH + head * HEAD_DIM
            x = total[:, begin : begin + HEAD_DIM]
            out_ref[:, begin : begin + HEAD_DIM] = (
                x.astype(bf16) if kind is None else head_norm(x, gain_ref[kind : kind + 1])
            )


def project(pairs, qk_gain, columns, name, starts=None, kinds=None, total=None):
    lefts, rights = [list(side) for side in zip(*pairs)]
    rows = lefts[0].shape[0]
    depth = sum(right.shape[0] for right in rights)
    resumed = total is not None
    operands = [qk_gain, *lefts, *rights] + [total] * resumed
    return pl.pallas_call(
        functools.partial(project_kernel, len(pairs), starts, kinds, columns, resumed),
        in_specs=[VMEM] * len(operands),
        out_specs=VMEM,
        out_shape=jax.ShapeDtypeStruct((rows, columns[1]), f32 if kinds is None else bf16),
        compiler_params=params(),
        cost_estimate=pl.CostEstimate(
            flops=2 * rows * depth * columns[1],
            bytes_accessed=2 * depth * (rows + columns[1]),
            transcendentals=rows,
        ),
        name=name,
    )(*operands)


def arrange_kernel(starts, order, homes, normed_ref, *out_refs):
    rows = normed_ref.shape[0]
    places, cores = starts()
    depth = normed_ref.shape[1] // lax.axis_size("fsdp")
    quarter = depth // 4
    source = lax.broadcasted_iota(jnp.int32, (depth, depth), 0)
    target = lax.broadcasted_iota(jnp.int32, (depth, depth), 1)
    for here in range(2):
        wanted = target
        for i, number in enumerate(order(cores[here])):
            inside = (target >= i * quarter) & (target < (i + 1) * quarter)
            wanted = jnp.where(inside, target + (number - i) * quarter, wanted)
        chosen = (source == wanted).astype(f32).astype(bf16)
        for slot, place in enumerate(places[here]):
            strip = normed_ref[:, pl.ds(pl.multiple_of(place, TILE), depth)]
            moved = dot(strip, chosen).astype(bf16)
            for i, (out, at) in enumerate(homes[slot]):
                out_refs[2 * out + here][:, at * quarter : (at + 1) * quarter] = moved[
                    :, i * quarter : (i + 1) * quarter
                ]


def arrange(starts, order, homes, widths, normed):
    rows = normed.shape[0]
    shapes = [jax.ShapeDtypeStruct((rows, width), bf16) for width in widths for _ in range(2)]
    return pl.pallas_call(
        functools.partial(arrange_kernel, starts, order, homes),
        in_specs=[VMEM],
        out_specs=[VMEM] * len(shapes),
        out_shape=shapes,
        compiler_params=params(),
        cost_estimate=pl.CostEstimate(
            flops=8 * rows * normed.shape[1] * TILE, bytes_accessed=4 * rows * normed.shape[1],
            transcendentals=0,
        ),
        name="arrange",
    )(normed)


def heads():
    for head in range(HEADS):
        ks = slice(head * HEAD_DIM, (head + 1) * HEAD_DIM)
        yield ks, slice(WIDTH + head * HEAD_DIM, WIDTH + (head + 1) * HEAD_DIM)


def share(query, keys, values, flag=None):
    raised = jnp.exp(dot_t(query, keys) * (1.0 / math.sqrt(HEAD_DIM)))
    if flag is not None:
        raised = raised * flag
    return dot(raised.astype(bf16), values), jnp.sum(raised, axis=-1, keepdims=True)


def edge_span(tile, tiles, ahead):
    if ahead:
        return slice(0, max(tile + REACH + 1 - tiles, 0) * TILE)
    return slice(BORDER - max(REACH - tile, 0) * TILE, BORDER)


def edge_share(queries_ref, edge_ref, tile, tiles, ahead, ks, vs, flag=None):
    span = edge_span(tile, tiles, ahead)
    if span.start == span.stop:
        return None
    query = queries_ref[tile * TILE : (tile + 1) * TILE, ks]
    return share(query, edge_ref[span, ks], edge_ref[span, vs], flag)


def attend_own_kernel(queries_ref, stacked_ref, near_ref, weighted_ref, mass_ref):
    tiles = queries_ref.shape[0] // TILE
    place = lax.axis_index("frame")
    inside = ((place ^ 1) < lax.axis_size("frame")).astype(f32)
    for odd in (0, 1):

        @pl.when((place & 1) == odd)
        def _():
            for ks, vs in heads():
                for tile in range(tiles):
                    rows = slice(tile * TILE, (tile + 1) * TILE)
                    span = slice(max(tile - REACH, 0) * TILE, min(tile + REACH + 1, tiles) * TILE)
                    keys, values = stacked_ref[span, ks], stacked_ref[span, vs]
                    weighted, mass = share(queries_ref[rows, ks], keys, values)
                    more = edge_share(queries_ref, near_ref, tile, tiles, odd == 0, ks, vs, inside)
                    if more is not None:
                        weighted, mass = weighted + more[0], mass + more[1]
                    weighted_ref[rows, ks] = weighted
                    mass_ref[rows, ks] = jnp.broadcast_to(mass, (TILE, HEAD_DIM))


def attend_own(queries, stacked, near):
    rows = queries.shape[0]
    return pl.pallas_call(
        attend_own_kernel,
        in_specs=[VMEM] * 3,
        out_specs=[VMEM] * 2,
        out_shape=[jax.ShapeDtypeStruct((rows, WIDTH), f32)] * 2,
        compiler_params=params(),
        cost_estimate=pl.CostEstimate(
            flops=4 * rows * rows * WIDTH, bytes_accessed=14 * rows * WIDTH,
            transcendentals=rows * rows * HEADS,
        ),
        name="attend_own_slab",
    )(queries, stacked, near)


def mix(layout, sources, attended, rows, blocks, sems, mixed_ref):
    width, copies = blocks.shape[2], []
    for number, (source, begin, place) in enumerate(layout()):
        held = sources[source][:, begin : begin + width]
        blocks[number, rows] = dot(attended[rows], held).astype(bf16)
        copy = pltpu.make_async_copy(
            blocks.at[number, rows],
            mixed_ref.at[0, rows, pl.ds(pl.multiple_of(place, TILE), width)],
            sems.at[number],
        )
        copy.start()
        copies.append(copy)
    return copies


def attend_kernel(layout, count, arrivals, queries_ref, weighted_ref, mass_ref, *refs):
    arrived, refs = refs[:arrivals], refs[arrivals:]
    sources = refs[:count]
    mixed_ref, far, attended, blocks, sems, late_sems = refs[count:]
    tiles = queries_ref.shape[0] // TILE
    place = lax.axis_index("frame")
    parity = place & 1
    exists = jnp.where(parity == 1, place < lax.axis_size("frame") - 1, place > 0)

    @pl.when(jnp.logical_not(exists))
    def _():
        attended[...] = (weighted_ref[...] / mass_ref[...]).astype(bf16)
        whole = slice(0, tiles * TILE)
        for copy in mix(layout, sources, attended, whole, blocks, sems, mixed_ref):
            copy.wait()

    for odd in (0, 1):
        spans = [edge_span(tile, tiles, odd == 1) for tile in range(tiles)]
        waiting = [tile for tile in range(tiles) if spans[tile].start != spans[tile].stop]
        ready = [tile for tile in range(tiles) if tile not in waiting]

        @pl.when(jnp.logical_and(exists, parity == odd))
        def _():
            copies = []
            if ready:
                rows = slice(ready[0] * TILE, (ready[-1] + 1) * TILE)
                attended[rows] = (weighted_ref[rows] / mass_ref[rows]).astype(bf16)
                copies += mix(layout, sources, attended, rows, blocks, sems, mixed_ref)
            total = arrived[0][...]
            for ref in arrived[1:]:
                total = total + ref[...]
            far[...] = total
            for ks, vs in heads():
                for tile in waiting:
                    rows = slice(tile * TILE, (tile + 1) * TILE)
                    more, extra = edge_share(queries_ref, far, tile, tiles, odd == 1, ks, vs)
                    weighted, mass = weighted_ref[rows, ks] + more, mass_ref[rows, ks] + extra
                    attended[rows, ks] = (weighted / mass).astype(bf16)
            rows = slice(waiting[0] * TILE, (waiting[-1] + 1) * TILE)
            copies += mix(layout, sources, attended, rows, blocks, late_sems, mixed_ref)
            for copy in copies:
                copy.wait()


def attend(layout, sources, queries, own, arrived, model):
    rows, number = queries.shape[0], len(layout())
    width = model // number
    return pl.pallas_call(
        functools.partial(attend_kernel, layout, len(sources), len(arrived)),
        in_specs=[VMEM] * (3 + len(arrived) + len(sources)),
        out_specs=ANY,
        out_shape=jax.ShapeDtypeStruct((1, rows, model), bf16),
        scratch_shapes=[
            pltpu.VMEM((BORDER, 2 * WIDTH), bf16),
            pltpu.VMEM((rows, WIDTH), bf16),
            pltpu.VMEM((number, rows, width), bf16),
            pltpu.SemaphoreType.DMA((number,)),
            pltpu.SemaphoreType.DMA((number,)),
        ],
        compiler_params=params(),
        cost_estimate=pl.CostEstimate(
            flops=2 * rows * WIDTH * (model + 4 * TILE),
            bytes_accessed=2 * (rows * model + WIDTH * model),
            transcendentals=rows * HEADS * 2 * TILE,
        ),
        name="attend_and_mix",
    )(queries, *own, *arrived, *sources)


def swap(x, axis, bits):
    return lax.ppermute(x, axis, [(i, i ^ bits) for i in range(lax.axis_size(axis))])


def swap_plane(x, turn):
    places = lax.axis_size("frame")
    pairs = []
    for i in range(lax.axis_size("fsdp")):
        for j in range(places):
            pairs.append((i * places + j, i * places + (j ^ (1 + (i + turn) % 2))))
    return lax.ppermute(x, ("fsdp", "frame"), pairs)


def hop_order(chips):
    odd = [k for k in range(chips - 1, 0, -1) if k % 2]
    return odd + [k - 1 for k in odd if k > 1]


def halos(stacked):
    places = lax.axis_size("frame")
    odd = lax.axis_index("frame") & 1
    tail = stacked.shape[0] - BORDER
    near = lax.dynamic_slice_in_dim(stacked, (1 - odd) * tail, BORDER, 0)
    far = lax.dynamic_slice_in_dim(stacked, odd * tail, BORDER, 0)
    axes = ("fsdp", "frame")
    straight, out, on = [], [], []
    for i in range(lax.axis_size("fsdp")):
        for j in range(0, places - 3, 4):
            for source, way, target in ((1, 3, 2), (2, 0, 1)):
                place = i * places + j
                if i % 2:
                    out.append((place + source, place + way))
                    on.append((place + way, place + target))
                else:
                    straight.append((place + source, place + target))
    way = lax.ppermute(far, axes, out)
    arrived = [lax.ppermute(way, axes, on), lax.ppermute(far, axes, straight)]
    rest = [j for j in range(1, places - 1, 2) if j % 4 == 3 or j >= places // 4 * 4]
    if rest:
        arrived.append(
            lax.ppermute(far, "frame", [(j, j + 1) for j in rest] + [(j + 1, j) for j in rest])
        )
    near_pairs = [(j, j ^ 1) for j in range(places) if j ^ 1 < places]
    return [lax.ppermute(near, "frame", near_pairs)] + arrived, way


def split_plan(frames, modulation, w_qkv, w_out, qk_gain):
    chips = lax.axis_size("fsdp") // 2
    shard_rows, columns = w_qkv.shape
    shard_columns = w_out.shape[1]
    quarter = shard_rows // 4
    hops = hop_order(chips)
    odd, even = [k for k in hops if k % 2], [k for k in hops if k % 2 == 0]
    front, back = [k for k in odd if k > 1], even
    ring = [1] + front + back
    fence = lax.optimization_barrier

    def where():
        place, index = lax.axis_index("frame"), lax.axis_index("fsdp")
        high = (place >> 1) & 1
        return index // 2, index % 2, 2 * ((place & 1) ^ high) + high

    def order(core):
        spot = where()[2]
        return spot, spot ^ (2 + core), spot ^ (3 - core), spot ^ 1

    def shard_places():
        chip, core, _ = where()
        cores = (core, 1 - core)
        return [[((chip ^ k) * 2 + c) * shard_rows for k in ring] for c in cores], cores

    def own_places():
        chip, core, _ = where()
        return [pl.multiple_of((2 * chip + c) * shard_rows, TILE) for c in (core, 1 - core)]

    def out_layout():
        chip, core, _ = where()
        place = 2 * chip + core
        return [
            (source, 0, (place ^ (2 * k + here)) * shard_columns)
            for source, (k, here) in enumerate((k, here) for k in [0] + ring for here in (0, 1))
        ]

    spot = where()[2]
    part = lax.dynamic_slice_in_dim(w_qkv, spot * quarter, quarter, 0)
    come = [swap(part, "fsdp", 2 * k) for k in front]
    near = swap(part, "fsdp", 2)
    other_qkv = swap(w_qkv, "fsdp", 1)
    normed = norm_rows(frames, modulation)
    normed, come = fence((normed, come))

    late = [swap(x, "fsdp", 2) for x in come]
    one = jnp.concatenate(come, axis=0)
    one_rest = swap_plane(one, 0)
    nf, nb = len(front), len(back)
    homes = [[(0, 2 * nf + nb), (0, 2 * nf + nb + 2), (1, 2 * nf + nb), (0, 2 * nf + nb + 1)]]
    homes += [[(0, i), (0, nf + i), (1, i), (1, nf + i)] for i in range(nf)]
    homes += [[(0, 2 * nf + i), (2, i), (1, 2 * nf + i), (2, nb + i)] for i in range(nb)]
    widths = [quarter * n for n in (2 * nf + nb + 3, 2 * nf + nb + 1, 2 * nb)]
    arranged = arrange(shard_places, order, homes, widths, normed)
    next_part = lax.dynamic_slice_in_dim(w_qkv, (spot ^ 1) * quarter, quarter, 0)
    one, one_rest, late, near, arranged, next_part = fence(
        (one, one_rest, late, near, arranged, next_part)
    )

    late = jnp.concatenate(late + [near], axis=0)
    two = swap_plane(jnp.concatenate([one, one_rest, late], axis=0), 1)
    near_rest = swap_plane(near, 0)
    across = swap(next_part, "fsdp", 2)
    cut = 7 * WIDTH // 8
    wides = [swap(w_out[:cut], "fsdp", 2 * k) for k in front]
    total = project(
        [(normed, w_qkv), (normed, other_qkv)], qk_gain, (0, columns), "project_own", own_places
    )
    two, near_rest, across, late, one, one_rest, wides, total = fence(
        (two, near_rest, across, late, one, one_rest, wides, total)
    )

    relayed = two[2 * nf * quarter : (2 * nf + nb) * quarter]
    three = swap_plane(jnp.concatenate([late[: nb * quarter], relayed], axis=0), 0)
    narrows = [swap(w_out[cut:], "fsdp", 2 * k) for k in front]
    kept = jnp.concatenate([one, one_rest, late, across, near_rest], axis=0)
    pieces = [kept, swap(kept, "fsdp", 1), two, swap(two, "fsdp", 1)]
    total = project(
        list(zip(arranged[:4], pieces)), qk_gain, (0, columns), "project_mid", total=total
    )
    other_out = swap(w_out, "fsdp", 1)
    total, three, narrows, other_out = fence((total, three, narrows, other_out))

    last = [(arranged[4], three), (arranged[5], swap(three, "fsdp", 1))]
    stacked = project(
        last, qk_gain, (WIDTH, 2 * WIDTH), "project_keys_values", kinds=(1, None), total=total
    )
    queries = project(last, qk_gain, (0, WIDTH), "project_queries", kinds=(0,), total=total)

    joined = [jnp.concatenate(pair, axis=0) for pair in zip(wides, narrows)]
    sources = [w_out, other_out]
    edges, way = halos(stacked)
    for x in [swap(w_out, "fsdp", 2)] + joined + [swap(x, "fsdp", 2) for x in joined]:
        sources += [x, swap(fence((x, way))[0], "fsdp", 1)]
    return queries, stacked, edges, out_layout, sources


def whole_plan(frames, modulation, w_qkv, w_out, qk_gain):
    rows = lax.all_gather(w_qkv, "fsdp", axis=0, tiled=True)
    columns = lax.all_gather(w_out, "fsdp", axis=1, tiled=True)
    normed = norm_rows(frames, modulation)
    stacked = project(
        [(normed, rows)], qk_gain, (WIDTH, 2 * WIDTH), "project_keys_values", kinds=(1, None)
    )
    queries = project([(normed, rows)], qk_gain, (0, WIDTH), "project_queries", kinds=(0,))
    return queries, stacked, halos(stacked)[0], lambda: [(0, i, i) for i in range(0, columns.shape[1], 3 * TILE)], [columns]


def on_device(frames, modulation, w_qkv, qk_gain, w_out):
    devices, places = lax.axis_size("fsdp"), lax.axis_size("frame")
    chips = devices // 2
    split = (
        devices % 2 == 0
        and chips > 2
        and chips & (chips - 1) == 0
        and w_qkv.shape[0] % TILE == 0
        and w_out.shape[1] % TILE == 0
    )
    plan = split_plan if split else whole_plan
    queries, stacked, edges, layout, sources = plan(
        frames[0], modulation[0], w_qkv, w_out, qk_gain
    )
    own = attend_own(queries, stacked, edges[0])
    return attend(layout, sources, queries, own, edges[1:], frames.shape[2])


def solution(mesh):
    return jax.shard_map(
        on_device,
        mesh=mesh,
        in_specs=(
            P("fsdp", "frame", None),
            P("fsdp", None, None),
            P("fsdp", None),
            P(),
            P(None, "fsdp"),
        ),
        out_specs=P("fsdp", "frame", None),
        check_vma=False,
    )
```

```python
import functools
import math

import jax
import jax.numpy as jnp
from jax import lax
from jax.experimental import pallas as pl
from jax.experimental.pallas import tpu as pltpu
from jax.sharding import PartitionSpec as P

HEAD_DIM = 128
HEADS = 2
WIDTH = HEADS * HEAD_DIM
TILE = 128
REACH = 2
BORDER = REACH * TILE
VMEM_BYTES = 40 * 1024 * 1024

f32 = jnp.float32
bf16 = jnp.bfloat16
ANY = pl.BlockSpec(memory_space=pl.ANY)
VMEM = pl.BlockSpec(memory_space=pltpu.VMEM)


def params():
    return pltpu.CompilerParams(vmem_limit_bytes=VMEM_BYTES)


def dot(a, b):
    return jnp.dot(a, b, preferred_element_type=f32)


def dot_t(a, b):
    return lax.dot_general(a, b, (((1,), (1,)), ((), ())), preferred_element_type=f32)


def norm_kernel(frames_ref, modulation_ref, normed_ref):
    values = frames_ref[...].astype(f32)
    average = jnp.mean(values, axis=-1, keepdims=True)
    centered = values - average
    spread = jnp.mean(centered * centered, axis=-1, keepdims=True)
    normed = centered * lax.rsqrt(spread + 1e-06)
    normed_ref[...] = (normed * (1.0 + modulation_ref[0:1]) + modulation_ref[1:2]).astype(bf16)


def norm_rows(frames, modulation):
    rows, width = frames.shape
    block = TILE // 2
    return pl.pallas_call(
        norm_kernel,
        grid=(rows // block,),
        in_specs=[
            pl.BlockSpec((block, width), lambda i: (i, 0)),
            pl.BlockSpec((2, width), lambda i: (0, 0)),
        ],
        out_specs=pl.BlockSpec((block, width), lambda i: (i, 0)),
        out_shape=jax.ShapeDtypeStruct((rows, width), bf16),
        compiler_params=params(),
        cost_estimate=pl.CostEstimate(
            flops=10 * rows * width, bytes_accessed=4 * rows * width, transcendentals=rows
        ),
        name="layer_norm",
    )(frames, modulation)


def head_norm(x, gain_row):
    squares = jnp.mean(x * x, axis=-1, keepdims=True)
    return (x * lax.rsqrt(squares + 1e-06) * gain_row).astype(bf16)


def project_kernel(count, starts, kinds, columns, resumed, gain_ref, *refs):
    lefts, rights = refs[:count], refs[count : 2 * count]
    total_ref, refs = refs[2 * count] if resumed else None, refs[2 * count + resumed :]
    out_ref = refs[0]
    first, number = columns
    total = total_ref[:, first : first + number] if resumed else None
    for i in range(count):
        depth = rights[i].shape[0]
        left = lefts[i][...] if starts is None else lefts[i][:, pl.ds(starts()[i], depth)]
        part = dot(left, rights[i][:, first : first + number])
        total = part if total is None else total + part
    if kinds is None:
        out_ref[...] = total
        return
    for block, kind in enumerate(kinds):
        for head in range(HEADS):
            begin = block * WIDTH + head * HEAD_DIM
            x = total[:, begin : begin + HEAD_DIM]
            out_ref[:, begin : begin + HEAD_DIM] = (
                x.astype(bf16) if kind is None else head_norm(x, gain_ref[kind : kind + 1])
            )


def project(pairs, qk_gain, columns, name, starts=None, kinds=None, total=None):
    lefts, rights = [list(side) for side in zip(*pairs)]
    rows = lefts[0].shape[0]
    depth = sum(right.shape[0] for right in rights)
    resumed = total is not None
    operands = [qk_gain, *lefts, *rights] + [total] * resumed
    return pl.pallas_call(
        functools.partial(project_kernel, len(pairs), starts, kinds, columns, resumed),
        in_specs=[VMEM] * len(operands),
        out_specs=VMEM,
        out_shape=jax.ShapeDtypeStruct((rows, columns[1]), f32 if kinds is None else bf16),
        compiler_params=params(),
        cost_estimate=pl.CostEstimate(
            flops=2 * rows * depth * columns[1],
            bytes_accessed=2 * depth * (rows + columns[1]),
            transcendentals=rows,
        ),
        name=name,
    )(*operands)


def arrange_kernel(starts, order, homes, normed_ref, *out_refs):
    rows = normed_ref.shape[0]
    places, cores = starts()
    depth = normed_ref.shape[1] // lax.axis_size("fsdp")
    quarter = depth // 4
    source = lax.broadcasted_iota(jnp.int32, (depth, depth), 0)
    target = lax.broadcasted_iota(jnp.int32, (depth, depth), 1)
    for here in range(2):
        wanted = target
        for i, number in enumerate(order(cores[here])):
            inside = (target >= i * quarter) & (target < (i + 1) * quarter)
            wanted = jnp.where(inside, target + (number - i) * quarter, wanted)
        chosen = (source == wanted).astype(f32).astype(bf16)
        for slot, place in enumerate(places[here]):
            strip = normed_ref[:, pl.ds(pl.multiple_of(place, TILE), depth)]
            moved = dot(strip, chosen).astype(bf16)
            for i, (out, at) in enumerate(homes[slot]):
                out_refs[2 * out + here][:, at * quarter : (at + 1) * quarter] = moved[
                    :, i * quarter : (i + 1) * quarter
                ]


def arrange(starts, order, homes, widths, normed):
    rows = normed.shape[0]
    shapes = [jax.ShapeDtypeStruct((rows, width), bf16) for width in widths for _ in range(2)]
    return pl.pallas_call(
        functools.partial(arrange_kernel, starts, order, homes),
        in_specs=[VMEM],
        out_specs=[VMEM] * len(shapes),
        out_shape=shapes,
        compiler_params=params(),
        cost_estimate=pl.CostEstimate(
            flops=8 * rows * normed.shape[1] * TILE, bytes_accessed=4 * rows * normed.shape[1],
            transcendentals=0,
        ),
        name="arrange",
    )(normed)


def heads():
    for head in range(HEADS):
        ks = slice(head * HEAD_DIM, (head + 1) * HEAD_DIM)
        yield ks, slice(WIDTH + head * HEAD_DIM, WIDTH + (head + 1) * HEAD_DIM)


def share(query, keys, values, flag=None):
    raised = jnp.exp(dot_t(query, keys) * (1.0 / math.sqrt(HEAD_DIM)))
    if flag is not None:
        raised = raised * flag
    return dot(raised.astype(bf16), values), jnp.sum(raised, axis=-1, keepdims=True)


def edge_span(tile, tiles, ahead):
    if ahead:
        return slice(0, max(tile + REACH + 1 - tiles, 0) * TILE)
    return slice(BORDER - max(REACH - tile, 0) * TILE, BORDER)


def edge_share(queries_ref, edge_ref, tile, tiles, ahead, ks, vs, flag=None):
    span = edge_span(tile, tiles, ahead)
    if span.start == span.stop:
        return None
    query = queries_ref[tile * TILE : (tile + 1) * TILE, ks]
    return share(query, edge_ref[span, ks], edge_ref[span, vs], flag)


def attend_own_kernel(queries_ref, stacked_ref, near_ref, weighted_ref, mass_ref):
    tiles = queries_ref.shape[0] // TILE
    place = lax.axis_index("frame")
    inside = ((place ^ 1) < lax.axis_size("frame")).astype(f32)
    for odd in (0, 1):

        @pl.when((place & 1) == odd)
        def _():
            for ks, vs in heads():
                for tile in range(tiles):
                    rows = slice(tile * TILE, (tile + 1) * TILE)
                    span = slice(max(tile - REACH, 0) * TILE, min(tile + REACH + 1, tiles) * TILE)
                    keys, values = stacked_ref[span, ks], stacked_ref[span, vs]
                    weighted, mass = share(queries_ref[rows, ks], keys, values)
                    more = edge_share(queries_ref, near_ref, tile, tiles, odd == 0, ks, vs, inside)
                    if more is not None:
                        weighted, mass = weighted + more[0], mass + more[1]
                    weighted_ref[rows, ks] = weighted
                    mass_ref[rows, ks] = jnp.broadcast_to(mass, (TILE, HEAD_DIM))


def attend_own(queries, stacked, near):
    rows = queries.shape[0]
    return pl.pallas_call(
        attend_own_kernel,
        in_specs=[VMEM] * 3,
        out_specs=[VMEM] * 2,
        out_shape=[jax.ShapeDtypeStruct((rows, WIDTH), f32)] * 2,
        compiler_params=params(),
        cost_estimate=pl.CostEstimate(
            flops=4 * rows * rows * WIDTH, bytes_accessed=14 * rows * WIDTH,
            transcendentals=rows * rows * HEADS,
        ),
        name="attend_own_slab",
    )(queries, stacked, near)


def mix(layout, sources, attended, rows, blocks, sems, mixed_ref):
    width, copies = blocks.shape[2], []
    for number, (source, begin, place) in enumerate(layout()):
        held = sources[source][:, begin : begin + width]
        blocks[number, rows] = dot(attended[rows], held).astype(bf16)
        copy = pltpu.make_async_copy(
            blocks.at[number, rows],
            mixed_ref.at[0, rows, pl.ds(pl.multiple_of(place, TILE), width)],
            sems.at[number],
        )
        copy.start()
        copies.append(copy)
    return copies


def attend_kernel(layout, count, arrivals, queries_ref, weighted_ref, mass_ref, *refs):
    arrived, refs = refs[:arrivals], refs[arrivals:]
    sources = refs[:count]
    mixed_ref, far, attended, blocks, sems, late_sems = refs[count:]
    tiles = queries_ref.shape[0] // TILE
    place = lax.axis_index("frame")
    parity = place & 1
    exists = jnp.where(parity == 1, place < lax.axis_size("frame") - 1, place > 0)

    @pl.when(jnp.logical_not(exists))
    def _():
        attended[...] = (weighted_ref[...] / mass_ref[...]).astype(bf16)
        whole = slice(0, tiles * TILE)
        for copy in mix(layout, sources, attended, whole, blocks, sems, mixed_ref):
            copy.wait()

    for odd in (0, 1):
        spans = [edge_span(tile, tiles, odd == 1) for tile in range(tiles)]
        waiting = [tile for tile in range(tiles) if spans[tile].start != spans[tile].stop]
        ready = [tile for tile in range(tiles) if tile not in waiting]

        @pl.when(jnp.logical_and(exists, parity == odd))
        def _():
            copies = []
            if ready:
                rows = slice(ready[0] * TILE, (ready[-1] + 1) * TILE)
                attended[rows] = (weighted_ref[rows] / mass_ref[rows]).astype(bf16)
                copies += mix(layout, sources, attended, rows, blocks, sems, mixed_ref)
            total = arrived[0][...]
            for ref in arrived[1:]:
                total = total + ref[...]
            far[...] = total
            for ks, vs in heads():
                for tile in waiting:
                    rows = slice(tile * TILE, (tile + 1) * TILE)
                    more, extra = edge_share(queries_ref, far, tile, tiles, odd == 1, ks, vs)
                    weighted, mass = weighted_ref[rows, ks] + more, mass_ref[rows, ks] + extra
                    attended[rows, ks] = (weighted / mass).astype(bf16)
            rows = slice(waiting[0] * TILE, (waiting[-1] + 1) * TILE)
            copies += mix(layout, sources, attended, rows, blocks, late_sems, mixed_ref)
            for copy in copies:
                copy.wait()


def attend(layout, sources, queries, own, arrived, model):
    rows, number = queries.shape[0], len(layout())
    width = model // number
    return pl.pallas_call(
        functools.partial(attend_kernel, layout, len(sources), len(arrived)),
        in_specs=[VMEM] * (3 + len(arrived) + len(sources)),
        out_specs=ANY,
        out_shape=jax.ShapeDtypeStruct((1, rows, model), bf16),
        scratch_shapes=[
            pltpu.VMEM((BORDER, 2 * WIDTH), bf16),
            pltpu.VMEM((rows, WIDTH), bf16),
            pltpu.VMEM((number, rows, width), bf16),
            pltpu.SemaphoreType.DMA((number,)),
            pltpu.SemaphoreType.DMA((number,)),
        ],
        compiler_params=params(),
        cost_estimate=pl.CostEstimate(
            flops=2 * rows * WIDTH * (model + 4 * TILE),
            bytes_accessed=2 * (rows * model + WIDTH * model),
            transcendentals=rows * HEADS * 2 * TILE,
        ),
        name="attend_and_mix",
    )(queries, *own, *arrived, *sources)


def swap(x, axis, bits):
    return lax.ppermute(x, axis, [(i, i ^ bits) for i in range(lax.axis_size(axis))])


def swap_plane(x, turn):
    places = lax.axis_size("frame")
    pairs = []
    for i in range(lax.axis_size("fsdp")):
        for j in range(places):
            pairs.append((i * places + j, i * places + (j ^ (1 + (i + turn) % 2))))
    return lax.ppermute(x, ("fsdp", "frame"), pairs)


def hop_order(chips):
    odd = [k for k in range(chips - 1, 0, -1) if k % 2]
    return odd + [k - 1 for k in odd if k > 1]


def halos(stacked):
    places = lax.axis_size("frame")
    odd = lax.axis_index("frame") & 1
    tail = stacked.shape[0] - BORDER
    near = lax.dynamic_slice_in_dim(stacked, (1 - odd) * tail, BORDER, 0)
    far = lax.dynamic_slice_in_dim(stacked, odd * tail, BORDER, 0)
    axes = ("fsdp", "frame")
    straight, out, on = [], [], []
    for i in range(lax.axis_size("fsdp")):
        for j in range(0, places - 3, 4):
            for source, way, target in ((1, 3, 2), (2, 0, 1)):
                place = i * places + j
                if i % 2:
                    out.append((place + source, place + way))
                    on.append((place + way, place + target))
                else:
                    straight.append((place + source, place + target))
    way = lax.ppermute(far, axes, out)
    arrived = [lax.ppermute(way, axes, on), lax.ppermute(far, axes, straight)]
    rest = [j for j in range(1, places - 1, 2) if j % 4 == 3 or j >= places // 4 * 4]
    if rest:
        arrived.append(
            lax.ppermute(far, "frame", [(j, j + 1) for j in rest] + [(j + 1, j) for j in rest])
        )
    near_pairs = [(j, j ^ 1) for j in range(places) if j ^ 1 < places]
    return [lax.ppermute(near, "frame", near_pairs)] + arrived, way


def split_plan(frames, modulation, w_qkv, w_out, qk_gain):
    chips = lax.axis_size("fsdp") // 2
    shard_rows, columns = w_qkv.shape
    shard_columns = w_out.shape[1]
    quarter = shard_rows // 4
    hops = hop_order(chips)
    odd, even = [k for k in hops if k % 2], [k for k in hops if k % 2 == 0]
    front, back = [k for k in odd if k > 1], even
    ring = [1] + front + back
    fence = lax.optimization_barrier

    def where():
        place, index = lax.axis_index("frame"), lax.axis_index("fsdp")
        high = (place >> 1) & 1
        return index // 2, index % 2, 2 * ((place & 1) ^ high) + high

    def order(core):
        spot = where()[2]
        return spot, spot ^ (2 + core), spot ^ (3 - core), spot ^ 1

    def shard_places():
        chip, core, _ = where()
        cores = (core, 1 - core)
        return [[((chip ^ k) * 2 + c) * shard_rows for k in ring] for c in cores], cores

    def own_places():
        chip, core, _ = where()
        return [pl.multiple_of((2 * chip + c) * shard_rows, TILE) for c in (core, 1 - core)]

    def out_layout():
        chip, core, _ = where()
        place = 2 * chip + core
        return [
            (source, 0, (place ^ (2 * k + here)) * shard_columns)
            for source, (k, here) in enumerate((k, here) for k in [0] + ring for here in (0, 1))
        ]

    spot = where()[2]
    part = lax.dynamic_slice_in_dim(w_qkv, spot * quarter, quarter, 0)
    come = [swap(part, "fsdp", 2 * k) for k in front]
    near = swap(part, "fsdp", 2)
    other_qkv = swap(w_qkv, "fsdp", 1)
    normed = norm_rows(frames, modulation)
    normed, come = fence((normed, come))

    late = [swap(x, "fsdp", 2) for x in come]
    one = jnp.concatenate(come, axis=0)
    one_rest = swap_plane(one, 0)
    nf, nb = len(front), len(back)
    homes = [[(0, 2 * nf + nb), (0, 2 * nf + nb + 2), (1, 2 * nf + nb), (0, 2 * nf + nb + 1)]]
    homes += [[(0, i), (0, nf + i), (1, i), (1, nf + i)] for i in range(nf)]
    homes += [[(0, 2 * nf + i), (2, i), (1, 2 * nf + i), (2, nb + i)] for i in range(nb)]
    widths = [quarter * n for n in (2 * nf + nb + 3, 2 * nf + nb + 1, 2 * nb)]
    arranged = arrange(shard_places, order, homes, widths, normed)
    next_part = lax.dynamic_slice_in_dim(w_qkv, (spot ^ 1) * quarter, quarter, 0)
    one, one_rest, late, near, arranged, next_part = fence(
        (one, one_rest, late, near, arranged, next_part)
    )

    late = jnp.concatenate(late + [near], axis=0)
    two = swap_plane(jnp.concatenate([one, one_rest, late], axis=0), 1)
    near_rest = swap_plane(near, 0)
    across = swap(next_part, "fsdp", 2)
    cut = 15 * WIDTH // 16
    wides = [swap(w_out[:cut], "fsdp", 2 * k) for k in front]
    total = project(
        [(normed, w_qkv), (normed, other_qkv)], qk_gain, (0, columns), "project_own", own_places
    )
    two, near_rest, across, late, one, one_rest, wides, total = fence(
        (two, near_rest, across, late, one, one_rest, wides, total)
    )

    relayed = two[2 * nf * quarter : (2 * nf + nb) * quarter]
    three = swap_plane(jnp.concatenate([late[: nb * quarter], relayed], axis=0), 0)
    narrows = [swap(w_out[cut:], "fsdp", 2 * k) for k in front]
    kept = jnp.concatenate([one, one_rest, late, across, near_rest], axis=0)
    pieces = [kept, swap(kept, "fsdp", 1), two, swap(two, "fsdp", 1)]
    total = project(
        list(zip(arranged[:4], pieces)), qk_gain, (0, columns), "project_mid", total=total
    )
    other_out = swap(w_out, "fsdp", 1)
    total, three, narrows, other_out = fence((total, three, narrows, other_out))

    last = [(arranged[4], three), (arranged[5], swap(three, "fsdp", 1))]
    stacked = project(
        last, qk_gain, (WIDTH, 2 * WIDTH), "project_keys_values", kinds=(1, None), total=total
    )
    queries = project(last, qk_gain, (0, WIDTH), "project_queries", kinds=(0,), total=total)

    joined = [jnp.concatenate(pair, axis=0) for pair in zip(wides, narrows)]
    sources = [w_out, other_out]
    edges, way = halos(stacked)
    for x in [swap(w_out, "fsdp", 2)] + joined + [swap(x, "fsdp", 2) for x in joined]:
        sources += [x, swap(fence((x, way))[0], "fsdp", 1)]
    return queries, stacked, edges, out_layout, sources


def whole_plan(frames, modulation, w_qkv, w_out, qk_gain):
    rows = lax.all_gather(w_qkv, "fsdp", axis=0, tiled=True)
    columns = lax.all_gather(w_out, "fsdp", axis=1, tiled=True)
    normed = norm_rows(frames, modulation)
    stacked = project(
        [(normed, rows)], qk_gain, (WIDTH, 2 * WIDTH), "project_keys_values", kinds=(1, None)
    )
    queries = project([(normed, rows)], qk_gain, (0, WIDTH), "project_queries", kinds=(0,))
    return queries, stacked, halos(stacked)[0], lambda: [(0, i, i) for i in range(0, columns.shape[1], 3 * TILE)], [columns]


def on_device(frames, modulation, w_qkv, qk_gain, w_out):
    devices, places = lax.axis_size("fsdp"), lax.axis_size("frame")
    chips = devices // 2
    split = (
        devices % 2 == 0
        and chips > 2
        and chips & (chips - 1) == 0
        and w_qkv.shape[0] % TILE == 0
        and w_out.shape[1] % TILE == 0
    )
    plan = split_plan if split else whole_plan
    queries, stacked, edges, layout, sources = plan(
        frames[0], modulation[0], w_qkv, w_out, qk_gain
    )
    own = attend_own(queries, stacked, edges[0])
    return attend(layout, sources, queries, own, edges[1:], frames.shape[2])


def solution(mesh):
    return jax.shard_map(
        on_device,
        mesh=mesh,
        in_specs=(
            P("fsdp", "frame", None),
            P("fsdp", None, None),
            P("fsdp", None),
            P(),
            P(None, "fsdp"),
        ),
        out_specs=P("fsdp", "frame", None),
        check_vma=False,
    )
```
